32 devices in a mesh: seq: 16 (over z, y, core), pair: 2 (over x).
Axes of the slice: x: 2, y: 2, z: 4, core: 2. Of those that a mesh axis runs over, the one named last changes fastest.
Arguments:
- student: float32 [10240, 1408], P('seq'), may hold values from -640 to 640
- teacher: float32 [10240, 1408], P('seq'), may hold values from -640 to 640
Outputs:
- student_grad: float32 [10240, 1408], P('seq')
The draws below stay inside these ranges and needn't reach their ends.
All inputs are finite; a program needn't handle non-finite values.
Results may differ from the reference program's by a relative error of at most 0.0059.
Values may be sent and summed in bfloat16 or wider, within the bound.
No kernel may reach another device: no remote copies, remote signals or barrier semaphores. Data moves between devices by JAX's collectives and lax.ppermute only.
A program may use at most 64 MiB of HBM per device.

```python
import math
import jax
import jax.numpy as jnp
from jax import lax

D = 1408
TOK_DEV = 640
TOKENS = 10240
N_SEQ = 16


def draw_student(key, part):
    key = jax.random.fold_in(key, 11)
    row_key, col_key, value_key = jax.random.split(key, 3)
    rows = jnp.exp(jax.random.uniform(row_key, (TOKENS, 1), jnp.float32, 0.0, math.log(10.0)))
    values = jnp.clip(jax.random.normal(value_key, (TOKENS, D), jnp.float32), -4.0, 4.0)
    cols = jnp.exp(jax.random.uniform(col_key, (1, D), jnp.float32, 0.0, math.log(10.0)))
    return values * rows * cols


def draw_teacher(key, part):
    key = jax.random.fold_in(key, 23)
    row_key, col_key, value_key = jax.random.split(key, 3)
    rows = jnp.exp(jax.random.uniform(row_key, (TOKENS, 1), jnp.float32, 0.0, math.log(10.0)))
    values = jnp.clip(jax.random.normal(value_key, (TOKENS, D), jnp.float32), -4.0, 4.0)
    cols = jnp.exp(jax.random.uniform(col_key, (1, D), jnp.float32, 0.0, math.log(10.0)))
    return values * rows * cols


def setup_inputs(seed: int = 0) -> dict:
    arg_keys = jax.random.split(jax.random.key(seed), 3)
    student = draw_student(jax.random.fold_in(arg_keys[2], 71), 0)
    teacher = draw_teacher(jax.random.fold_in(arg_keys[2], 71), 0)
    return dict(student=student, teacher=teacher)


def normalize(values, width):
    scale = lax.rsqrt(lax.optimization_barrier(jnp.sum(values * values, axis=1, keepdims=True)) + width * 1e-06)
    return (scale, values * scale)

def relation_block(own_s, own_t, all_s, all_t, margin, weight):
    s_rel = jnp.dot(own_s, all_s.T, preferred_element_type=jnp.float32)
    t_rel = jnp.dot(own_t, all_t.T, preferred_element_type=jnp.float32)
    delta = s_rel - t_rel
    shrink = jnp.maximum(delta - margin, 0.0) + jnp.minimum(delta + margin, 0.0)
    relation = (weight * shrink).astype(jnp.bfloat16)
    return jnp.dot(relation, all_s, preferred_element_type=jnp.float32)

def reference(student, teacher):
    s_scale, s_unit = normalize(student, D)
    t_scale, t_unit = normalize(teacher, D)
    s_half = s_unit.astype(jnp.bfloat16)
    t_half = t_unit.astype(jnp.bfloat16)
    margin = 0.75 / math.sqrt(D)
    weight = 64.0 * D / math.sqrt(TOKENS)
    blocks = (s_half.reshape(N_SEQ, TOK_DEV, D), t_half.reshape(N_SEQ, TOK_DEV, D))

    def one_block(pair_rows):
        return relation_block(pair_rows[0], pair_rows[1], s_half, t_half, margin, weight)
    unit_grad = lax.map(one_block, blocks).reshape(TOKENS, D)
    dotted = lax.optimization_barrier(jnp.sum(s_unit * unit_grad, axis=1, keepdims=True))
    return s_scale * (unit_grad - s_unit * dotted)
```

```python
import math

import jax
import jax.numpy as jnp
from jax import lax
from jax.sharding import PartitionSpec as P

CHUNKS = 2


def normalize(values, width):
    scale = lax.rsqrt(jnp.sum(values * values, axis=1, keepdims=True) + width * 1e-06)
    return (scale, values * scale)


def relation_tile(own_s, own_t, partner_s, partner_t, margin, weight):
    contract = (((1,), (1,)), ((), ()))
    s_rel = lax.dot_general(own_s, partner_s, contract, preferred_element_type=jnp.float32)
    t_rel = lax.dot_general(own_t, partner_t, contract, preferred_element_type=jnp.float32)
    delta = s_rel - t_rel
    shrink = jnp.maximum(delta - margin, 0.0) + jnp.minimum(delta + margin, 0.0)
    relation = (weight * shrink).astype(jnp.bfloat16)
    return jnp.dot(relation, partner_s, preferred_element_type=jnp.float32)


def project(unit, grad):
    return grad - unit * jnp.sum(unit * grad, axis=1, keepdims=True)


def sum_over_pair(value, count):
    distance = 1
    while distance < count:
        half = value.astype(jnp.bfloat16)
        other = lax.ppermute(half, "pair", [(i, i ^ distance) for i in range(count)])
        value = half.astype(jnp.float32) + other.astype(jnp.float32)
        distance *= 2
    return value


def local(student, teacher):
    rows, width = student.shape
    seq_count = lax.axis_size("seq")
    pair_count = lax.axis_size("pair")
    pair_index = lax.axis_index("pair")
    margin = 0.75 / math.sqrt(width)
    weight = 64.0 * width / math.sqrt(rows * seq_count)
    s_scale, s_unit = normalize(student, width)
    t_scale, t_unit = normalize(teacher, width)
    s_half = s_unit.astype(jnp.bfloat16)
    t_half = t_unit.astype(jnp.bfloat16)
    share = rows // pair_count
    piece = share // CHUNKS

    total = jnp.zeros((rows, width), jnp.float32)
    for chunk in range(CHUNKS):
        start = pair_index * share + chunk * piece
        s_part = lax.dynamic_slice_in_dim(s_half, start, piece, 0)
        t_part = lax.dynamic_slice_in_dim(t_half, start, piece, 0)
        all_s = lax.all_gather(s_part, "seq", axis=0, tiled=True)
        all_t = lax.all_gather(t_part, "seq", axis=0, tiled=True)
        total = total + relation_tile(s_half, t_half, all_s, all_t, margin, weight)
    return s_scale * sum_over_pair(project(s_unit, total), pair_count)


def solution(mesh):
    placed = (P("seq", None), P("seq", None))
    return jax.shard_map(
        local, mesh=mesh, in_specs=placed, out_specs=P("seq", None), check_vma=False
    )
```

```python
import math

import jax
import jax.numpy as jnp
from jax import lax
from jax.sharding import PartitionSpec as P

CORES = 2


def normalize(values, width):
    scale = lax.rsqrt(jnp.sum(values * values, axis=1, keepdims=True) + width * 1e-06)
    return (scale, values * scale)


def relation_tile(own_s, own_t, partner_s, partner_t, margin, weight):
    contract = (((1,), (1,)), ((), ()))
    s_rel = lax.dot_general(own_s, partner_s, contract, preferred_element_type=jnp.float32)
    t_rel = lax.dot_general(own_t, partner_t, contract, preferred_element_type=jnp.float32)
    delta = s_rel - t_rel
    shrink = jnp.maximum(delta - margin, 0.0) + jnp.minimum(delta + margin, 0.0)
    relation = (weight * shrink).astype(jnp.bfloat16)
    return jnp.dot(relation, partner_s, preferred_element_type=jnp.float32)


def project(unit, grad):
    return grad - unit * jnp.sum(unit * grad, axis=1, keepdims=True)


def sum_over_pair(value, count):
    distance = 1
    while distance < count:
        half = value.astype(jnp.bfloat16)
        other = lax.ppermute(half, "pair", [(i, i ^ distance) for i in range(count)])
        value = half.astype(jnp.float32) + other.astype(jnp.float32)
        distance *= 2
    return value


def ring_routes(count):
    chips = count // CORES
    order = list(range(0, chips, 2)) + list(range(1, chips, 2))[::-1]
    onward, back = [], []
    for place, chip in enumerate(order):
        following = order[(place + 1) % chips]
        for core in range(CORES):
            onward.append((chip * CORES + core, following * CORES + core))
            back.append((following * CORES + core, chip * CORES + core))
    swap = [(i, i ^ 1) for i in range(count)]
    return onward, back, swap


def local(student, teacher):
    rows, width = student.shape
    seq_count = lax.axis_size("seq")
    pair_count = lax.axis_size("pair")
    pair_index = lax.axis_index("pair")
    margin = 0.75 / math.sqrt(width)
    weight = 64.0 * width / math.sqrt(rows * seq_count)
    s_scale, s_unit = normalize(student, width)
    t_scale, t_unit = normalize(teacher, width)
    s_half = s_unit.astype(jnp.bfloat16)
    t_half = t_unit.astype(jnp.bfloat16)
    share = rows // pair_count
    onward, back, swap = ring_routes(seq_count)

    def send(parts, route):
        return tuple(lax.ppermute(part, "seq", route) for part in parts)

    def tile(parts):
        return relation_tile(s_half, t_half, parts[0], parts[1], margin, weight)

    start = pair_index * share
    own = tuple(lax.dynamic_slice_in_dim(x, start, share, 0) for x in (s_half, t_half))
    total = tile(own) + tile(send(own, swap))
    streams = [(own, onward), (own, back)]
    for hop in range(1, seq_count // CORES // 2 + 1):
        if hop == seq_count // CORES // 2:
            streams = [
                (tuple(x[: share // 2] for x in streams[0][0]), onward),
                (tuple(x[share // 2 :] for x in streams[1][0]), back),
            ]
        streams = [(send(parts, route), route) for parts, route in streams]
        for parts, _ in streams:
            total = total + tile(parts) + tile(send(parts, swap))
    return s_scale * sum_over_pair(project(s_unit, total), pair_count)


def solution(mesh):
    placed = (P("seq", None), P("seq", None))
    return jax.shard_map(
        local, mesh=mesh, in_specs=placed, out_specs=P("seq", None), check_vma=False
    )
```

```python
import functools
import math

import jax
import jax.numpy as jnp
from jax import lax
from jax.experimental import pallas as pl
from jax.experimental.pallas import tpu as pltpu
from jax.sharding import PartitionSpec as P

CORES = 2
ROW_TILE = 16
VMEM_LIMIT = 48 * 1024 * 1024


def normalize(values, width):
    scale = lax.rsqrt(jnp.sum(values * values, axis=1, keepdims=True) + width * 1e-06)
    return (scale, values * scale)


def relation_kernel(margin, weight, counts, has_total, last, *refs):
    refs = list(refs)
    own_s, own_t = refs[:2]
    partners = refs[2 : 2 + 2 * len(counts)]
    rest = refs[2 + 2 * len(counts) :]
    total = rest.pop(0) if has_total else None
    student, scale = (rest.pop(0), rest.pop(0)) if last else (None, None)
    out, all_s, all_t = rest

    @pl.when(pl.program_id(0) == 0)
    def _():
        at = 0
        for k, count in enumerate(counts):
            all_s[at : at + count, :] = partners[2 * k][...]
            all_t[at : at + count, :] = partners[2 * k + 1][...]
            at += count

    contract = (((1,), (1,)), ((), ()))
    s_rel = lax.dot_general(own_s[...], all_s[...], contract, preferred_element_type=jnp.float32)
    t_rel = lax.dot_general(own_t[...], all_t[...], contract, preferred_element_type=jnp.float32)
    delta = s_rel - t_rel
    shrink = jnp.maximum(delta - margin, 0.0) + jnp.minimum(delta + margin, 0.0)
    relation = (weight * shrink).astype(jnp.bfloat16)
    grad = jnp.dot(relation, all_s[...], preferred_element_type=jnp.float32)
    if has_total:
        grad = total[...] + grad
    if last:
        unit = student[...] * scale[...]
        grad = grad - unit * jnp.sum(unit * grad, axis=1, keepdims=True)
    out[...] = grad.astype(out.dtype)


def add_relation(own, partners, total, final, margin, weight):
    rows, width = own[0].shape
    block = rows // 2
    counts = tuple(s.shape[0] for s, _ in partners)
    tokens = sum(counts)
    flat = [x for pair in partners for x in pair]
    by_row = pl.BlockSpec((block, width), lambda i: (i, 0))
    operands = list(own) + flat
    specs = [by_row, by_row] + [
        pl.BlockSpec(x.shape, lambda i: (0, 0), pipeline_mode=pl.Buffered(1)) for x in flat
    ]
    aliases = {}
    if total is not None:
        if final is None:
            aliases = {len(operands): 0}
        operands.append(total)
        specs.append(by_row)
    if final is not None:
        operands += list(final)
        specs += [by_row, pl.BlockSpec((block, 1), lambda i: (i, 0))]
    dtype = jnp.float32 if final is None else jnp.bfloat16
    return pl.pallas_call(
        functools.partial(
            relation_kernel, margin, weight, counts, total is not None, final is not None
        ),
        grid=(rows // block,),
        in_specs=specs,
        out_specs=by_row,
        out_shape=jax.ShapeDtypeStruct((rows, width), dtype),
        scratch_shapes=[pltpu.VMEM((tokens, width), jnp.bfloat16)] * 2,
        input_output_aliases=aliases,
        compiler_params=pltpu.CompilerParams(vmem_limit_bytes=VMEM_LIMIT),
        cost_estimate=pl.CostEstimate(
            flops=6 * rows * tokens * width,
            bytes_accessed=4 * rows * width + 4 * tokens * width + 8 * rows * width,
            transcendentals=0,
        ),
    )(*operands)


def sum_over_pair(half, count):
    distance = 1
    value = half
    while distance < count:
        half = value.astype(jnp.bfloat16)
        other = lax.ppermute(half, "pair", [(i, i ^ distance) for i in range(count)])
        value = half.astype(jnp.float32) + other.astype(jnp.float32)
        distance *= 2
    return value


def ring_routes(count):
    chips = count // CORES
    order = list(range(0, chips, 2)) + list(range(1, chips, 2))[::-1]
    onward, back = [], []
    for place, chip in enumerate(order):
        following = order[(place + 1) % chips]
        for core in range(CORES):
            onward.append((chip * CORES + core, following * CORES + core))
            back.append((following * CORES + core, chip * CORES + core))
    swap = [(i, i ^ 1) for i in range(count)]
    return onward, back, swap


def local(student, teacher):
    rows, width = student.shape
    seq_count = lax.axis_size("seq")
    pair_count = lax.axis_size("pair")
    pair_index = lax.axis_index("pair")
    margin = 0.75 / math.sqrt(width)
    weight = 64.0 * width / math.sqrt(rows * seq_count)
    s_scale, s_unit = normalize(student, width)
    t_scale, t_unit = normalize(teacher, width)
    s_half = s_unit.astype(jnp.bfloat16)
    t_half = t_unit.astype(jnp.bfloat16)
    share = rows // pair_count
    first = -(-share // (2 * ROW_TILE)) * ROW_TILE
    onward, back, swap = ring_routes(seq_count)

    def send(parts, route):
        return tuple(lax.ppermute(part, "seq", route) for part in parts)

    def add(partners, total, final=None):
        return add_relation((s_half, t_half), partners, total, final, margin, weight)

    start = pair_index * share
    own = tuple(lax.dynamic_slice_in_dim(x, start, share, 0) for x in (s_half, t_half))
    total = add([own, send(own, swap)], None)
    onto, off = own, own
    hops = seq_count // CORES // 2
    for hop in range(1, hops + 1):
        final = None
        if hop == hops:
            onto = tuple(x[:first] for x in onto)
            off = tuple(x[first:] for x in off)
            final = (student, s_scale)
        onto, off = send(onto, onward), send(off, back)
        total = add([onto, off, send(onto, swap), send(off, swap)], total, final)
    return s_scale * sum_over_pair(total, pair_count)


def solution(mesh):
    placed = (P("seq", None), P("seq", None))
    return jax.shard_map(
        local, mesh=mesh, in_specs=placed, out_specs=P("seq", None), check_vma=False
    )
```

```python
import functools
import math

import jax
import jax.numpy as jnp
from jax import lax
from jax.experimental import pallas as pl
from jax.experimental.pallas import tpu as pltpu
from jax.sharding import PartitionSpec as P

CORES = 2
ROW_TILE = 16
VMEM_LIMIT = 32 * 1024 * 1024


def normalize(values, width):
    scale = lax.rsqrt(jnp.sum(values * values, axis=1, keepdims=True) + width * 1e-06)
    return (scale, values * scale)


def relation_kernel(margin, weight, counts, has_total, project, *refs):
    refs = list(refs)
    own_s, own_t = refs[:2]
    partners = refs[2 : 2 + len(counts)]
    rest = refs[2 + len(counts) :]
    total = rest.pop(0) if has_total else None
    student, scale = (rest.pop(0), rest.pop(0)) if project else (None, None)
    out, all_s, all_t = rest

    @pl.when(pl.program_id(0) == 0)
    def _():
        at = 0
        for partner, count in zip(partners, counts):
            all_s[at : at + count, :] = partner[:count, :]
            all_t[at : at + count, :] = partner[count:, :]
            at += count

    contract = (((1,), (1,)), ((), ()))
    s_rel = lax.dot_general(own_s[...], all_s[...], contract, preferred_element_type=jnp.float32)
    t_rel = lax.dot_general(own_t[...], all_t[...], contract, preferred_element_type=jnp.float32)
    delta = s_rel - t_rel
    shrink = jnp.maximum(delta - margin, 0.0) + jnp.minimum(delta + margin, 0.0)
    relation = (weight * shrink).astype(jnp.bfloat16)
    grad = jnp.dot(relation, all_s[...], preferred_element_type=jnp.float32)
    if has_total:
        grad = total[...] + grad
    if project:
        unit = student[...] * scale[...]
        grad = grad - unit * jnp.sum(unit * grad, axis=1, keepdims=True)
    out[...] = grad.astype(out.dtype)


def add_relation(own, partners, total, margin, weight, project=None, dtype=jnp.float32):
    rows, width = own[0].shape
    block = rows // 2
    counts = tuple(x.shape[0] // 2 for x in partners)
    tokens = sum(counts)
    by_row = pl.BlockSpec((block, width), lambda i: (i, 0))
    operands = list(own) + list(partners)
    specs = [by_row, by_row] + [
        pl.BlockSpec(x.shape, lambda i: (0, 0), pipeline_mode=pl.Buffered(1)) for x in partners
    ]
    aliases = {}
    if total is not None:
        if dtype == total.dtype:
            aliases = {len(operands): 0}
        operands.append(total)
        specs.append(by_row)
    if project is not None:
        operands += list(project)
        specs += [by_row, pl.BlockSpec((block, 1), lambda i: (i, 0))]
    return pl.pallas_call(
        functools.partial(
            relation_kernel, margin, weight, counts, total is not None, project is not None
        ),
        grid=(rows // block,),
        in_specs=specs,
        out_specs=by_row,
        out_shape=jax.ShapeDtypeStruct((rows, width), dtype),
        scratch_shapes=[pltpu.VMEM((tokens, width), jnp.bfloat16)] * 2,
        input_output_aliases=aliases,
        compiler_params=pltpu.CompilerParams(vmem_limit_bytes=VMEM_LIMIT),
        cost_estimate=pl.CostEstimate(
            flops=6 * rows * tokens * width,
            bytes_accessed=4 * rows * width + 4 * tokens * width + 8 * rows * width,
            transcendentals=0,
        ),
    )(*operands)


def ring_routes(count):
    chips = count // CORES
    order = list(range(0, chips, 2)) + list(range(1, chips, 2))[::-1]
    onward, back = [], []
    for place, chip in enumerate(order):
        following = order[(place + 1) % chips]
        for core in range(CORES):
            onward.append((chip * CORES + core, following * CORES + core))
            back.append((following * CORES + core, chip * CORES + core))
    swap = [(i, i ^ 1) for i in range(count)]
    return onward, back, swap


def halves(tokens):
    first = -(-tokens // (2 * ROW_TILE)) * ROW_TILE
    return first, tokens - first


def local(student, teacher):
    rows, width = student.shape
    seq_count = lax.axis_size("seq")
    pair_count = lax.axis_size("pair")
    pair_index = lax.axis_index("pair")
    margin = 0.75 / math.sqrt(width)
    weight = 64.0 * width / math.sqrt(rows * seq_count)
    s_scale, s_unit = normalize(student, width)
    t_scale, t_unit = normalize(teacher, width)
    s_half = s_unit.astype(jnp.bfloat16)
    t_half = t_unit.astype(jnp.bfloat16)
    share = rows // pair_count
    onward, back, swap = ring_routes(seq_count)
    hops = seq_count // CORES // 2

    def send(groups):
        return [(way, [lax.ppermute(x, "seq", way) for x in xs]) for way, xs in groups]

    def swapped(groups):
        return [lax.ppermute(x, "seq", swap) for _, xs in groups for x in xs]

    def arrays(groups):
        return [x for _, xs in groups for x in xs]

    def after(groups, value):
        return [(way, [lax.optimization_barrier((x, value))[0] for x in xs]) for way, xs in groups]

    def add(partners, total, project=None, dtype=jnp.float32):
        return add_relation((s_half, t_half), partners, total, margin, weight, project, dtype)

    def add_groups(groups, total, project=None, dtype=jnp.float32):
        return add(arrays(groups) + swapped(groups), total, project, dtype)

    def piece(start, count):
        at = pair_index * share + start
        cut = lambda x: lax.dynamic_slice_in_dim(x, at, count, 0)
        return jnp.concatenate([cut(s_half), cut(t_half)])

    first, second = halves(share)
    own = [piece(0, first), piece(first, second)]

    def in_two(x):
        tokens = x.shape[0] // 2
        left, right = halves(tokens)
        cut = lambda at, count: jnp.concatenate([x[at : at + count], x[tokens + at : tokens + at + count]])
        return [cut(0, left), cut(left, right)]

    far = [(onward, in_two(own[0])), (back, in_two(own[1]))]
    near = [(onward, [own[1]]), (back, [own[0]])]
    waiting = [(onward, own)]
    total = None
    far = send(far)
    for hop in range(2, hops):
        total = add_groups(waiting, total)
        waiting = far
        if hop == hops - 1:
            near = after(after(near, total), far[0][1][0])
        far = send(after(far, total))
    near = send(near)
    total = add_groups(waiting, total)
    mine = after(far, total)
    theirs = [
        [
            (way, [lax.ppermute(x, "pair", [(i, (i + k) % pair_count) for i in range(pair_count)]) for x in xs])
            for way, xs in mine
        ]
        for k in range(1, pair_count)
    ]
    waiting = far
    for hop in range(2, hops):
        following = send(after(near, total))
        total = add_groups(waiting, total)
        waiting = near
        near = following
    last = after(send(after(mine, near[0][1][0])), total)
    total = add_groups(waiting, total)
    partial_grad = add_groups(near, total, (student, s_scale), jnp.bfloat16)
    summed = partial_grad.astype(jnp.float32)
    distance = 1
    while distance < pair_count:
        half = summed.astype(jnp.bfloat16)
        other = lax.ppermute(half, "pair", [(i, i ^ distance) for i in range(pair_count)])
        summed = half.astype(jnp.float32) + other.astype(jnp.float32)
        distance *= 2
    rest = [send(after(groups, partial_grad)) for groups in theirs]
    total = add_groups(last, None)
    for k, groups in enumerate(rest):
        final = (student, s_scale) if k == len(rest) - 1 else None
        total = add_groups(groups, total, final)
    return s_scale * (summed + total)


def solution(mesh):
    placed = (P("seq", None), P("seq", None))
    return jax.shard_map(
        local, mesh=mesh, in_specs=placed, out_specs=P("seq", None), check_vma=False
    )
```

```python
import functools
import math

import jax
import jax.numpy as jnp
from jax import lax
from jax.experimental import pallas as pl
from jax.experimental.pallas import tpu as pltpu
from jax.sharding import PartitionSpec as P

CORES = 2
ROW_TILE = 16
VMEM_LIMIT = 32 * 1024 * 1024


def normalized(values):
    width = values.shape[1]
    scale = lax.rsqrt(jnp.sum(values * values, axis=1, keepdims=True) + width * 1e-06)
    return scale, (values * scale).astype(jnp.bfloat16)


def own_kernel(student, teacher, half, scale):
    scale[...], half[0] = normalized(student[...])
    _, half[1] = normalized(teacher[...])


def normalize_own(student, teacher):
    rows, width = student.shape
    block = rows // 4
    by_row = pl.BlockSpec((block, width), lambda i: (i, 0))
    return pl.pallas_call(
        own_kernel,
        grid=(rows // block,),
        in_specs=[by_row, by_row],
        out_specs=[
            pl.BlockSpec((2, block, width), lambda i: (0, i, 0)),
            pl.BlockSpec((block, 1), lambda i: (i, 0)),
        ],
        out_shape=[
            jax.ShapeDtypeStruct((2, rows, width), jnp.bfloat16),
            jax.ShapeDtypeStruct((rows, 1), jnp.float32),
        ],
        compiler_params=pltpu.CompilerParams(vmem_limit_bytes=VMEM_LIMIT),
        cost_estimate=pl.CostEstimate(
            flops=6 * rows * width, bytes_accessed=12 * rows * width, transcendentals=2 * rows
        ),
    )(student, teacher)


def pack_kernel(counts, which, student, teacher, *packed):
    at = 0
    for out, count in zip(packed, counts):
        out[:count, :] = normalized(student[at : at + count, :])[1]
        out[count:, :] = normalized(teacher[at : at + count, :])[1]
        at += count


def pack_share(student, teacher, pair_index, counts):
    share, width = sum(counts), student.shape[1]
    mine = pl.BlockSpec((share, width), lambda i, which: (which[0], 0))
    return pl.pallas_call(
        functools.partial(pack_kernel, counts),
        grid_spec=pltpu.PrefetchScalarGridSpec(
            num_scalar_prefetch=1,
            grid=(1,),
            in_specs=[mine, mine],
            out_specs=[pl.BlockSpec((2 * n, width), lambda i, which: (0, 0)) for n in counts],
        ),
        out_shape=[jax.ShapeDtypeStruct((2 * n, width), jnp.bfloat16) for n in counts],
        compiler_params=pltpu.CompilerParams(vmem_limit_bytes=VMEM_LIMIT),
        cost_estimate=pl.CostEstimate(
            flops=6 * share * width, bytes_accessed=12 * share * width, transcendentals=2 * share
        ),
    )(jnp.reshape(pair_index, (1,)).astype(jnp.int32), student, teacher)


def relation_kernel(margin, weight, counts, terms, project, *refs):
    refs = list(refs)
    rows = refs.pop(0)
    partners = [refs.pop(0) for _ in counts]
    added = [refs.pop(0) for _ in range(terms)]
    student, scale = (refs.pop(0), refs.pop(0)) if project else (None, None)
    out, all_s, all_t = refs

    @pl.when(pl.program_id(0) == 0)
    def _():
        at = 0
        for partner, count in zip(partners, counts):
            all_s[at : at + count, :] = partner[:count, :]
            all_t[at : at + count, :] = partner[count:, :]
            at += count

    contract = (((1,), (1,)), ((), ()))
    s_rel = lax.dot_general(rows[0], all_s[...], contract, preferred_element_type=jnp.float32)
    t_rel = lax.dot_general(rows[1], all_t[...], contract, preferred_element_type=jnp.float32)
    delta = s_rel - t_rel
    shrink = jnp.maximum(delta - margin, 0.0) + jnp.minimum(delta + margin, 0.0)
    relation = (weight * shrink).astype(jnp.bfloat16)
    grad = jnp.dot(relation, all_s[...], preferred_element_type=jnp.float32)
    for term in added:
        grad = term[...] + grad
    if project:
        unit = student[...] * scale[...]
        grad = grad - unit * jnp.sum(unit * grad, axis=1, keepdims=True)
    out[...] = grad.astype(out.dtype)


def add_relation(half, partners, terms, margin, weight, project=None, dtype=jnp.float32):
    _, rows, width = half.shape
    block = rows // 2
    counts = tuple(x.shape[0] // 2 for x in partners)
    tokens = sum(counts)
    by_row = pl.BlockSpec((block, width), lambda i: (i, 0))
    operands = [half] + list(partners) + list(terms)
    specs = [pl.BlockSpec((2, block, width), lambda i: (0, i, 0))]
    specs += [pl.BlockSpec(x.shape, lambda i: (0, 0), pipeline_mode=pl.Buffered(1)) for x in partners]
    specs += [by_row] * len(terms)
    aliases = {1 + len(partners): 0} if terms and dtype == terms[0].dtype else {}
    if project is not None:
        operands += list(project)
        specs += [by_row, pl.BlockSpec((block, 1), lambda i: (i, 0))]
    return pl.pallas_call(
        functools.partial(relation_kernel, margin, weight, counts, len(terms), project is not None),
        grid=(rows // block,),
        in_specs=specs,
        out_specs=by_row,
        out_shape=jax.ShapeDtypeStruct((rows, width), dtype),
        scratch_shapes=[pltpu.VMEM((tokens, width), jnp.bfloat16)] * 2,
        input_output_aliases=aliases,
        compiler_params=pltpu.CompilerParams(vmem_limit_bytes=VMEM_LIMIT),
        cost_estimate=pl.CostEstimate(
            flops=6 * rows * tokens * width,
            bytes_accessed=(12 * rows + 4 * tokens) * width,
            transcendentals=0,
        ),
    )(*operands)


def ring_routes(count):
    chips = count // CORES
    order = list(range(0, chips, 2)) + list(range(1, chips, 2))[::-1]
    onward, back = [], []
    for place, chip in enumerate(order):
        following = order[(place + 1) % chips]
        for core in range(CORES):
            onward.append((chip * CORES + core, following * CORES + core))
            back.append((following * CORES + core, chip * CORES + core))
    swap = [(i, i ^ 1) for i in range(count)]
    return onward, back, swap


def halves(tokens):
    first = -(-tokens // (2 * ROW_TILE)) * ROW_TILE
    return first, tokens - first


def after(x, *values):
    return lax.optimization_barrier((x, *values))[0]


def local(student, teacher):
    rows, width = student.shape
    seq_count = lax.axis_size("seq")
    pair_count = lax.axis_size("pair")
    pair_index = lax.axis_index("pair")
    margin = 0.75 / math.sqrt(width)
    weight = 64.0 * width / math.sqrt(rows * seq_count)
    onward, back, swap = ring_routes(seq_count)
    hops = seq_count // CORES // 2
    counts = [n for part in halves(rows // pair_count) for n in halves(part)]
    pieces = pack_share(student, teacher, pair_index, counts)
    own_half, s_scale = normalize_own(student, teacher)
    other_half = lax.ppermute(own_half, "seq", swap)
    own, other = None, None

    def add(half, partners, terms, project=None, dtype=jnp.float32):
        return add_relation(half, partners, terms, margin, weight, project, dtype)

    def hop(chains, wait_for=()):
        sent = []
        for k, chain in enumerate(chains):
            if wait_for and k:
                chain = [after(x, *wait_for) for x in chain]
            sent.append([lax.ppermute(chain[0], "seq", onward), lax.ppermute(chain[1], "seq", back)])
        return sent

    def once(chains, arrived):
        return [[after(x, y) for x, y in zip(*both)] for both in zip(chains, arrived)]

    def flat(chains):
        return [x for chain in chains for x in chain]

    def terms(total):
        return [] if total is None else [total]

    far = [[pieces[0], pieces[2]], [pieces[1], pieces[3]]]
    near = [[pieces[2], pieces[0]], [pieces[3], pieces[1]]]
    batch = list(pieces)
    arrivals = []
    for step in range(1, hops):
        far = hop(far, () if own is None else (own, other))
        batch += flat(far)
        if step % 2 == 1 or step == hops - 1:
            other = add(other_half, batch, terms(other))
            own = add(own_half, batch, terms(own))
            batch = []
    near = once(near, far)
    theirs = []
    for k in range(1, pair_count):
        route = [(i, (i + k) % pair_count) for i in range(pair_count)]
        theirs.append([[lax.ppermute(x, "pair", route) for x in chain] for chain in far])
    for step in range(1, hops):
        near = hop(near, (own, other) if step % 2 == 0 else ())
        batch += flat(near)
        if step % 2 == 0 and step < hops - 1:
            other = add(other_half, batch, terms(other))
            own = add(own_half, batch, terms(own))
            batch = []
    far = hop(once(far, near), (own, other))
    other = add(other_half, batch, terms(other))
    moved = lax.ppermute(other, "seq", swap)
    partial_grad = add(own_half, batch, [own, moved], (student, s_scale), jnp.bfloat16)
    summed = partial_grad
    distance = 1
    while distance < pair_count:
        half = summed.astype(jnp.bfloat16)
        arrived = lax.ppermute(half, "pair", [(i, i ^ distance) for i in range(pair_count)])
        summed = half.astype(jnp.float32) + arrived.astype(jnp.float32)
        distance *= 2
    own, other = None, None
    for chains in theirs:
        batch = flat(far)
        far = hop(once(chains, far), (partial_grad,))
        other = add(other_half, batch, terms(other))
        own = add(own_half, batch, terms(own))
    batch = flat(far)
    other = add(other_half, batch, terms(other))
    moved = lax.ppermute(other, "seq", swap)
    total = add(own_half, batch, terms(own) + [moved], (student, s_scale))
    return s_scale * (summed + total)


def solution(mesh):
    placed = (P("seq", None), P("seq", None))
    return jax.shard_map(
        local, mesh=mesh, in_specs=placed, out_specs=P("seq", None), check_vma=False
    )
```

```python
import functools
import math

import jax
import jax.numpy as jnp
from jax import lax
from jax.experimental import pallas as pl
from jax.experimental.pallas import tpu as pltpu
from jax.sharding import PartitionSpec as P

CORES = 2
DOUBLED = 0
TIE_RELAY = (1,)
TIE_SWAP = (0, 1)
MERGE_FIRST = True
ROW_TILE = 16
VMEM_LIMIT = 32 * 1024 * 1024
FIRST_VMEM_LIMIT = 58 * 1024 * 1024


def normalized(values):
    width = values.shape[1]
    scale = lax.rsqrt(jnp.sum(values * values, axis=1, keepdims=True) + width * 1e-06)
    return scale, (values * scale).astype(jnp.bfloat16)


def own_kernel(student, teacher, half, scale):
    scale[...], half[0] = normalized(student[...])
    _, half[1] = normalized(teacher[...])


def normalize_own(student, teacher):
    rows, width = student.shape
    block = rows // 4
    by_row = pl.BlockSpec((block, width), lambda i: (i, 0))
    return pl.pallas_call(
        own_kernel,
        grid=(rows // block,),
        in_specs=[by_row, by_row],
        out_specs=[
            pl.BlockSpec((2, block, width), lambda i: (0, i, 0)),
            pl.BlockSpec((block, 1), lambda i: (i, 0)),
        ],
        out_shape=[
            jax.ShapeDtypeStruct((2, rows, width), jnp.bfloat16),
            jax.ShapeDtypeStruct((rows, 1), jnp.float32),
        ],
        compiler_params=pltpu.CompilerParams(vmem_limit_bytes=VMEM_LIMIT),
        cost_estimate=pl.CostEstimate(
            flops=6 * rows * width, bytes_accessed=12 * rows * width, transcendentals=2 * rows
        ),
    )(student, teacher)


def pack_kernel(counts, which, student, teacher, *packed):
    at = 0
    for out, count in zip(packed, counts):
        out[:count, :] = normalized(student[at : at + count, :])[1]
        out[count:, :] = normalized(teacher[at : at + count, :])[1]
        at += count


def pack_share(student, teacher, pair_index, share, counts):
    width = student.shape[1]
    mine = pl.BlockSpec((share, width), lambda i, which: (which[0], 0))
    return pl.pallas_call(
        functools.partial(pack_kernel, counts),
        grid_spec=pltpu.PrefetchScalarGridSpec(
            num_scalar_prefetch=1,
            grid=(1,),
            in_specs=[mine, mine],
            out_specs=[pl.BlockSpec((2 * n, width), lambda i, which: (0, 0)) for n in counts],
        ),
        out_shape=[jax.ShapeDtypeStruct((2 * n, width), jnp.bfloat16) for n in counts],
        compiler_params=pltpu.CompilerParams(vmem_limit_bytes=FIRST_VMEM_LIMIT),
        cost_estimate=pl.CostEstimate(
            flops=6 * share * width, bytes_accessed=12 * share * width, transcendentals=2 * share
        ),
    )(jnp.reshape(pair_index, (1,)).astype(jnp.int32), student, teacher)


def relation_kernel(margin, weight, counts, terms, project, halves, *refs):
    refs = list(refs)
    rows = refs.pop(0)
    partners = [refs.pop(0) for _ in counts]
    added = [refs.pop(0) for _ in range(terms)]
    student, scale = (refs.pop(0), refs.pop(0)) if project else (None, None)
    summands = [refs.pop(0) for _ in range(halves)]
    out, all_s, all_t = refs

    @pl.when(pl.program_id(0) == 0)
    def _():
        at = 0
        for partner, count in zip(partners, counts):
            all_s[at : at + count, :] = partner[:count, :]
            all_t[at : at + count, :] = partner[count:, :]
            at += count

    contract = (((1,), (1,)), ((), ()))
    s_rel = lax.dot_general(rows[0], all_s[...], contract, preferred_element_type=jnp.float32)
    t_rel = lax.dot_general(rows[1], all_t[...], contract, preferred_element_type=jnp.float32)
    delta = s_rel - t_rel
    shrink = jnp.maximum(delta - margin, 0.0) + jnp.minimum(delta + margin, 0.0)
    relation = (weight * shrink).astype(jnp.bfloat16)
    grad = jnp.dot(relation, all_s[...], preferred_element_type=jnp.float32)
    for term in added:
        grad = grad + term[...].astype(jnp.float32)
    if project:
        unit = student[...] * scale[...]
        grad = grad - unit * jnp.sum(unit * grad, axis=1, keepdims=True)
    if summands:
        others = [x[...].astype(jnp.float32) for x in summands]
        grad = scale[...] * (sum(others[1:], others[0]) + grad)
    out[...] = grad.astype(out.dtype)


def add_relation(half, partners, terms, margin, weight, project=None, summands=(), dtype=jnp.float32):
    _, rows, width = half.shape
    block = rows // 2
    counts = tuple(x.shape[0] // 2 for x in partners)
    tokens = sum(counts)
    by_row = pl.BlockSpec((block, width), lambda i: (i, 0))
    operands = [half] + list(partners) + list(terms)
    specs = [pl.BlockSpec((2, block, width), lambda i: (0, i, 0))]
    specs += [pl.BlockSpec(x.shape, lambda i: (0, 0), pipeline_mode=pl.Buffered(1)) for x in partners]
    specs += [by_row] * len(terms)
    aliases = {1 + len(partners): 0} if terms and dtype == terms[0].dtype else {}
    if project is not None:
        operands += list(project)
        specs += [by_row, pl.BlockSpec((block, 1), lambda i: (i, 0))]
    operands += list(summands)
    specs += [by_row] * len(summands)
    return pl.pallas_call(
        functools.partial(
            relation_kernel, margin, weight, counts, len(terms), project is not None, len(summands)
        ),
        grid=(rows // block,),
        in_specs=specs,
        out_specs=by_row,
        out_shape=jax.ShapeDtypeStruct((rows, width), dtype),
        scratch_shapes=[pltpu.VMEM((tokens, width), jnp.bfloat16)] * 2,
        input_output_aliases=aliases,
        compiler_params=pltpu.CompilerParams(vmem_limit_bytes=VMEM_LIMIT),
        cost_estimate=pl.CostEstimate(
            flops=6 * rows * tokens * width,
            bytes_accessed=(12 * rows + 4 * tokens) * width,
            transcendentals=0,
        ),
    )(*operands)


def ring_routes(count):
    chips = count // CORES
    order = list(range(0, chips, 2)) + list(range(1, chips, 2))[::-1]
    onward, back = [], []
    for place, chip in enumerate(order):
        following = order[(place + 1) % chips]
        for core in range(CORES):
            onward.append((chip * CORES + core, following * CORES + core))
            back.append((following * CORES + core, chip * CORES + core))
    swap = [(i, i ^ 1) for i in range(count)]
    return onward, back, swap


def split(tokens, parts):
    tiles = tokens // ROW_TILE
    return [ROW_TILE * (tiles // parts + (k < tiles % parts)) for k in range(parts)]


def after(x, *values):
    return lax.optimization_barrier((x, *values))[0] if values else x


def cut(piece, start, count):
    tokens = piece.shape[0] // 2
    return jnp.concatenate([piece[start : start + count], piece[tokens + start : tokens + start + count]])


def local(student, teacher):
    rows, width = student.shape
    seq_count = lax.axis_size("seq")
    pair_count = lax.axis_size("pair")
    pair_index = lax.axis_index("pair")
    margin = 0.75 / math.sqrt(width)
    weight = 64.0 * width / math.sqrt(rows * seq_count)
    onward, back, swap = ring_routes(seq_count)
    hops = seq_count // CORES // 2
    share = rows // pair_count
    doubled = max(1, round(DOUBLED * share / ROW_TILE)) * ROW_TILE if pair_count == 2 and DOUBLED else 0
    pieces = pack_share(student, teacher, pair_index, share, split(share - doubled, 2))
    own_half, s_scale = normalize_own(after(student, *pieces), teacher)

    def add(batch, total, **options):
        return add_relation(own_half, batch, [] if total is None else [total], margin, weight, **options)

    def hop(chains, wait_for=()):
        sent = []
        for k, (onto, off) in enumerate(chains):
            if k in TIE_RELAY:
                onto, off = after(onto, *wait_for), after(off, *wait_for)
            sent.append((lax.ppermute(onto, "seq", onward), lax.ppermute(off, "seq", back)))
        return sent

    def swapped(chains, wait_for=()):
        return [
            lax.ppermute(after(x, *wait_for) if k in TIE_SWAP else x, "seq", swap)
            for k, chain in enumerate(chains)
            for x in chain
        ]

    def flat(chains):
        return [x for chain in chains for x in chain]

    def last_cut(chains):
        cuts = []
        for k, (onto, off) in enumerate(chains):
            first, second = split(onto.shape[0] // 2, 2)
            if k % 2:
                first, second = second, first
            cuts.append((cut(onto, 0, first), cut(off, first, second)))
        return cuts

    def around(pieces, began, before, **options):
        chains = [(x, x) for x in pieces]
        batch = list(pieces) + [lax.ppermute(x, "seq", swap) for x in pieces]
        if began:
            chains = [(after(on, done[0]), after(off, done[1])) for (on, off), done in zip(chains, began)]
        total = None
        older = before
        for step in range(1, hops + 1):
            if step == hops:
                chains = last_cut(chains)
            chains = hop(chains, older)
            older = () if total is None else (total,)
            if batch and (step > 1 or not MERGE_FIRST):
                total = add(batch, total)
                batch = []
            batch += flat(chains) + swapped(chains, older if total is None else (total,))
        return chains, (total,), add(batch, total, **options)

    arrived, before, own = around(pieces, None, (), project=(student, s_scale), dtype=jnp.bfloat16)
    distance = 1
    summands = (own,)
    while distance < pair_count:
        value = sum(x.astype(jnp.float32) for x in summands).astype(jnp.bfloat16)
        route = [(i, i ^ distance) for i in range(pair_count)]
        summands = (value, lax.ppermute(value, "pair", route))
        distance *= 2
    if not doubled:
        return s_scale * sum(x.astype(jnp.float32) for x in summands)

    ends = own_half.reshape(2, pair_count, share, width)[:, :, share - doubled :]
    lasts, at = [], 0
    for n in split(doubled, 2):
        if n:
            lasts.append(ends[:, :, at : at + n].reshape(2 * pair_count * n, width))
        at += n
    _, _, result = around(lasts, arrived, (own,), project=(student, s_scale), summands=summands)
    return result


def solution(mesh):
    placed = (P("seq", None), P("seq", None))
    return jax.shard_map(
        local, mesh=mesh, in_specs=placed, out_specs=P("seq", None), check_vma=False
    )
```

```python
import functools
import math

import jax
import jax.numpy as jnp
from jax import lax
from jax.experimental import pallas as pl
from jax.experimental.pallas import tpu as pltpu
from jax.sharding import PartitionSpec as P

CORES = 2
PARTS = 4
CHAINS = 2
LAG = 2
SLAG = 1
FIRST = 2
COSTW = 1.0
ROW_TILE = 16
VMEM_LIMIT = 32 * 1024 * 1024
FIRST_VMEM_LIMIT = 58 * 1024 * 1024


def normalized(values):
    width = values.shape[1]
    scale = lax.rsqrt(jnp.sum(values * values, axis=1, keepdims=True) + width * 1e-06)
    return scale, (values * scale).astype(jnp.bfloat16)


def own_kernel(student, teacher, half, scale):
    scale[...], half[0] = normalized(student[...])
    _, half[1] = normalized(teacher[...])


def normalize_own(student, teacher):
    rows, width = student.shape
    block = rows // 4
    by_row = pl.BlockSpec((block, width), lambda i: (i, 0))
    return pl.pallas_call(
        own_kernel,
        grid=(rows // block,),
        in_specs=[by_row, by_row],
        out_specs=[
            pl.BlockSpec((2, block, width), lambda i: (0, i, 0)),
            pl.BlockSpec((block, 1), lambda i: (i, 0)),
        ],
        out_shape=[
            jax.ShapeDtypeStruct((2, rows, width), jnp.bfloat16),
            jax.ShapeDtypeStruct((rows, 1), jnp.float32),
        ],
        compiler_params=pltpu.CompilerParams(vmem_limit_bytes=VMEM_LIMIT),
        cost_estimate=pl.CostEstimate(
            flops=6 * rows * width, bytes_accessed=12 * rows * width, transcendentals=2 * rows
        ),
    )(student, teacher)


def pack_kernel(counts, which, student, teacher, *packed):
    at = 0
    for out, count in zip(packed, counts):
        out[:count, :] = normalized(student[at : at + count, :])[1]
        out[count:, :] = normalized(teacher[at : at + count, :])[1]
        at += count


def pack_share(student, teacher, pair_index, share, counts):
    width = student.shape[1]
    mine = pl.BlockSpec((share, width), lambda i, which: (which[0], 0))
    return pl.pallas_call(
        functools.partial(pack_kernel, counts),
        grid_spec=pltpu.PrefetchScalarGridSpec(
            num_scalar_prefetch=1,
            grid=(1,),
            in_specs=[mine, mine],
            out_specs=[pl.BlockSpec((2 * n, width), lambda i, which: (0, 0)) for n in counts],
        ),
        out_shape=[jax.ShapeDtypeStruct((2 * n, width), jnp.bfloat16) for n in counts],
        compiler_params=pltpu.CompilerParams(vmem_limit_bytes=FIRST_VMEM_LIMIT),
        cost_estimate=pl.CostEstimate(
            flops=6 * share * width, bytes_accessed=12 * share * width, transcendentals=2 * share
        ),
    )(jnp.reshape(pair_index, (1,)).astype(jnp.int32), student, teacher)


def relation_kernel(margin, weight, counts, terms, project, halves, *refs):
    refs = list(refs)
    rows = refs.pop(0)
    partners = [refs.pop(0) for _ in counts]
    added = [refs.pop(0) for _ in range(terms)]
    student, scale = (refs.pop(0), refs.pop(0)) if project else (None, None)
    summands = [refs.pop(0) for _ in range(halves)]
    out, all_s, all_t = refs

    @pl.when(pl.program_id(0) == 0)
    def _():
        at = 0
        for partner, count in zip(partners, counts):
            all_s[at : at + count, :] = partner[:count, :]
            all_t[at : at + count, :] = partner[count:, :]
            at += count

    contract = (((1,), (1,)), ((), ()))
    s_rel = lax.dot_general(rows[0], all_s[...], contract, preferred_element_type=jnp.float32)
    t_rel = lax.dot_general(rows[1], all_t[...], contract, preferred_element_type=jnp.float32)
    delta = s_rel - t_rel
    shrink = jnp.maximum(delta - margin, 0.0) + jnp.minimum(delta + margin, 0.0)
    relation = (weight * shrink).astype(jnp.bfloat16)
    grad = jnp.dot(relation, all_s[...], preferred_element_type=jnp.float32)
    for term in added:
        grad = grad + term[...].astype(jnp.float32)
    if project:
        unit = student[...] * scale[...]
        grad = grad - unit * jnp.sum(unit * grad, axis=1, keepdims=True)
    if summands:
        others = [x[...].astype(jnp.float32) for x in summands]
        grad = scale[...] * (sum(others[1:], others[0]) + grad)
    out[...] = grad.astype(out.dtype)


def add_relation(half, partners, terms, margin, weight, project=None, summands=(), dtype=jnp.float32):
    _, rows, width = half.shape
    block = rows // 2
    counts = tuple(x.shape[0] // 2 for x in partners)
    tokens = sum(counts)
    by_row = pl.BlockSpec((block, width), lambda i: (i, 0))
    operands = [half] + list(partners) + list(terms)
    specs = [pl.BlockSpec((2, block, width), lambda i: (0, i, 0))]
    specs += [pl.BlockSpec(x.shape, lambda i: (0, 0), pipeline_mode=pl.Buffered(1)) for x in partners]
    specs += [by_row] * len(terms)
    aliases = {1 + len(partners): 0} if terms and dtype == terms[0].dtype else {}
    if project is not None:
        operands += list(project)
        specs += [by_row, pl.BlockSpec((block, 1), lambda i: (i, 0))]
    operands += list(summands)
    specs += [by_row] * len(summands)
    return pl.pallas_call(
        functools.partial(
            relation_kernel, margin, weight, counts, len(terms), project is not None, len(summands)
        ),
        grid=(rows // block,),
        in_specs=specs,
        out_specs=by_row,
        out_shape=jax.ShapeDtypeStruct((rows, width), dtype),
        scratch_shapes=[pltpu.VMEM((tokens, width), jnp.bfloat16)] * 2,
        input_output_aliases=aliases,
        compiler_params=pltpu.CompilerParams(vmem_limit_bytes=VMEM_LIMIT),
        cost_estimate=pl.CostEstimate(
            flops=6 * rows * tokens * width,
            bytes_accessed=(12 * rows + 4 * tokens) * width,
            transcendentals=0,
        ),
    )(*operands)


def ring_routes(count):
    chips = count // CORES
    order = list(range(0, chips, 2)) + list(range(1, chips, 2))[::-1]
    around = []
    for place, chip in enumerate(order):
        following = order[(place + 1) % chips]
        around.append((chip * CORES, following * CORES))
        around.append((following * CORES + 1, chip * CORES + 1))
    return around, [(to, of) for of, to in around], [(i, i ^ 1) for i in range(count)]


def split(tokens, parts):
    tiles = tokens // ROW_TILE
    return [ROW_TILE * (tiles // parts + (k < tiles % parts)) for k in range(parts)]


def after(x, *values):
    return lax.optimization_barrier((x, *values))[0] if values else x


def local(student, teacher):
    rows, width = student.shape
    seq_count = lax.axis_size("seq")
    pair_count = lax.axis_size("pair")
    pair_index = lax.axis_index("pair")
    margin = 0.75 / math.sqrt(width)
    weight = 64.0 * width / math.sqrt(rows * seq_count)
    around, reverse, swap = ring_routes(seq_count)
    hops = seq_count // CORES - 2
    share = rows // pair_count
    pieces = list(pack_share(student, teacher, pair_index, share, split(share, CHAINS)))
    own_half, s_scale = normalize_own(after(student, *pieces), teacher)

    def add(batch, total, **options):
        return add_relation(own_half, batch, [] if total is None else [total], margin, weight, **options)

    def move(x, route, *wait_for):
        return lax.ppermute(after(x, *wait_for), "seq", route)

    batch = pieces + [move(x, swap) for x in pieces]
    totals = []
    held = list(pieces)
    doubled = pair_count == 2
    for event in range(CHAINS * hops):
        k = event % CHAINS
        held[k] = move(held[k], around, *(totals[-1 - LAG :][:1] if len(totals) > LAG else []))
        if event >= FIRST:
            totals.append(add(batch, totals[-1] if totals else None))
            batch = []
        batch += [held[k], move(held[k], swap, *totals[len(totals) - 1 - SLAG :][:1] if len(totals) > SLAG else [])]
    if not doubled:
        nearest = [move(x, reverse) for x in pieces]
        batch += nearest + [move(x, swap) for x in nearest]
    own = add(batch, totals[-1], project=(student, s_scale), dtype=jnp.bfloat16)
    distance = 1
    summands = (own,)
    while distance < pair_count:
        value = sum(x.astype(jnp.float32) for x in summands).astype(jnp.bfloat16)
        route = [(i, i ^ distance) for i in range(pair_count)]
        summands = (value, lax.ppermute(value, "pair", route))
        distance *= 2
    summed = sum(x.astype(jnp.float32) for x in summands)
    if not doubled:
        return s_scale * summed

    total, at, batch = None, 0, []
    nearest = []
    for k, n in enumerate(split(rows, PARTS)):
        part = own_half[:, at : at + n].reshape(2 * n, width)
        nearest.append(move(part, reverse, *([own] if k == PARTS - 1 else [held[k % CHAINS]])))
        at += n
    for x in nearest[:-1]:
        batch += [x, move(x, swap, own)]
    total = add(batch, None)
    batch = [nearest[-1], move(nearest[-1], swap, total, summands[-1])]
    total = add(batch, total, project=(student, s_scale))
    return s_scale * (summed + total)


def solution(mesh):
    placed = (P("seq", None), P("seq", None))
    return jax.shard_map(
        local, mesh=mesh, in_specs=placed, out_specs=P("seq", None), check_vma=False
    )
```

```python
import functools
import math

import jax
import jax.numpy as jnp
from jax import lax
from jax.experimental import pallas as pl
from jax.experimental.pallas import tpu as pltpu
from jax.sharding import PartitionSpec as P

CORES = 2
PARTS = 4
CHAINS = 2
LAG = 2
SLAG = 1
FIRST = 2
COSTW = 1.0
ROW_TILE = 16
VMEM_LIMIT = 32 * 1024 * 1024
FIRST_VMEM_LIMIT = 58 * 1024 * 1024


def normalized(values):
    width = values.shape[1]
    scale = lax.rsqrt(jnp.sum(values * values, axis=1, keepdims=True) + width * 1e-06)
    return scale, (values * scale).astype(jnp.bfloat16)


def own_kernel(student, teacher, half, scale):
    scale[...], half[0] = normalized(student[...])
    _, half[1] = normalized(teacher[...])


def normalize_own(student, teacher):
    rows, width = student.shape
    block = rows // 4
    by_row = pl.BlockSpec((block, width), lambda i: (i, 0))
    return pl.pallas_call(
        own_kernel,
        grid=(rows // block,),
        in_specs=[by_row, by_row],
        out_specs=[
            pl.BlockSpec((2, block, width), lambda i: (0, i, 0)),
            pl.BlockSpec((block, 1), lambda i: (i, 0)),
        ],
        out_shape=[
            jax.ShapeDtypeStruct((2, rows, width), jnp.bfloat16),
            jax.ShapeDtypeStruct((rows, 1), jnp.float32),
        ],
        compiler_params=pltpu.CompilerParams(vmem_limit_bytes=VMEM_LIMIT),
        cost_estimate=pl.CostEstimate(
            flops=6 * rows * width, bytes_accessed=12 * rows * width, transcendentals=2 * rows
        ),
    )(student, teacher)


def pack_kernel(counts, which, student, teacher, *packed):
    at = 0
    for out, count in zip(packed, counts):
        out[:count, :] = normalized(student[at : at + count, :])[1]
        out[count:, :] = normalized(teacher[at : at + count, :])[1]
        at += count


def pack_share(student, teacher, pair_index, share, counts):
    width = student.shape[1]
    mine = pl.BlockSpec((share, width), lambda i, which: (which[0], 0))
    return pl.pallas_call(
        functools.partial(pack_kernel, counts),
        grid_spec=pltpu.PrefetchScalarGridSpec(
            num_scalar_prefetch=1,
            grid=(1,),
            in_specs=[mine, mine],
            out_specs=[pl.BlockSpec((2 * n, width), lambda i, which: (0, 0)) for n in counts],
        ),
        out_shape=[jax.ShapeDtypeStruct((2 * n, width), jnp.bfloat16) for n in counts],
        compiler_params=pltpu.CompilerParams(vmem_limit_bytes=FIRST_VMEM_LIMIT),
        cost_estimate=pl.CostEstimate(
            flops=6 * share * width, bytes_accessed=12 * share * width, transcendentals=2 * share
        ),
    )(jnp.reshape(pair_index, (1,)).astype(jnp.int32), student, teacher)


def relation_kernel(margin, weight, counts, terms, project, halves, *refs):
    refs = list(refs)
    rows = refs.pop(0)
    partners = [refs.pop(0) for _ in counts]
    added = [refs.pop(0) for _ in range(terms)]
    student, scale = (refs.pop(0), refs.pop(0)) if project else (None, None)
    summands = [refs.pop(0) for _ in range(halves)]
    out, all_s, all_t = refs

    @pl.when(pl.program_id(0) == 0)
    def _():
        at = 0
        for partner, count in zip(partners, counts):
            all_s[at : at + count, :] = partner[:count, :]
            all_t[at : at + count, :] = partner[count:, :]
            at += count

    contract = (((1,), (1,)), ((), ()))
    s_rel = lax.dot_general(rows[0], all_s[...], contract, preferred_element_type=jnp.float32)
    t_rel = lax.dot_general(rows[1], all_t[...], contract, preferred_element_type=jnp.float32)
    delta = s_rel - t_rel
    shrink = jnp.maximum(delta - margin, 0.0) + jnp.minimum(delta + margin, 0.0)
    relation = (weight * shrink).astype(jnp.bfloat16)
    grad = jnp.dot(relation, all_s[...], preferred_element_type=jnp.float32)
    for term in added:
        grad = grad + term[...].astype(jnp.float32)
    if project:
        unit = student[...] * scale[...]
        grad = grad - unit * jnp.sum(unit * grad, axis=1, keepdims=True)
    if summands:
        others = [x[...].astype(jnp.float32) for x in summands]
        grad = scale[...] * (sum(others[1:], others[0]) + grad)
    out[...] = grad.astype(out.dtype)


def add_relation(half, partners, terms, margin, weight, project=None, summands=(), dtype=jnp.float32):
    _, rows, width = half.shape
    block = rows // 2
    counts = tuple(x.shape[0] // 2 for x in partners)
    tokens = sum(counts)
    by_row = pl.BlockSpec((block, width), lambda i: (i, 0))
    operands = [half] + list(partners) + list(terms)
    specs = [pl.BlockSpec((2, block, width), lambda i: (0, i, 0))]
    specs += [pl.BlockSpec(x.shape, lambda i: (0, 0), pipeline_mode=pl.Buffered(1)) for x in partners]
    specs += [by_row] * len(terms)
    aliases = {1 + len(partners): 0} if terms and dtype == terms[0].dtype else {}
    if project is not None:
        operands += list(project)
        specs += [by_row, pl.BlockSpec((block, 1), lambda i: (i, 0))]
    operands += list(summands)
    specs += [by_row] * len(summands)
    return pl.pallas_call(
        functools.partial(
            relation_kernel, margin, weight, counts, len(terms), project is not None, len(summands)
        ),
        grid=(rows // block,),
        in_specs=specs,
        out_specs=by_row,
        out_shape=jax.ShapeDtypeStruct((rows, width), dtype),
        scratch_shapes=[pltpu.VMEM((tokens, width), jnp.bfloat16)] * 2,
        input_output_aliases=aliases,
        compiler_params=pltpu.CompilerParams(vmem_limit_bytes=VMEM_LIMIT),
        cost_estimate=pl.CostEstimate(
            flops=6 * rows * tokens * width,
            bytes_accessed=(12 * rows + 4 * tokens) * width,
            transcendentals=0,
        ),
    )(*operands)


def ring_routes(count):
    chips = count // CORES
    order = list(range(0, chips, 2)) + list(range(1, chips, 2))[::-1]
    around = []
    for place, chip in enumerate(order):
        following = order[(place + 1) % chips]
        around.append((chip * CORES, following * CORES))
        around.append((following * CORES + 1, chip * CORES + 1))
    return around, [(to, of) for of, to in around], [(i, i ^ 1) for i in range(count)]


def split(tokens, parts):
    tiles = tokens // ROW_TILE
    return [ROW_TILE * (tiles // parts + (k < tiles % parts)) for k in range(parts)]


def after(x, *values):
    return lax.optimization_barrier((x, *values))[0] if values else x


def local(student, teacher):
    rows, width = student.shape
    seq_count = lax.axis_size("seq")
    pair_count = lax.axis_size("pair")
    pair_index = lax.axis_index("pair")
    margin = 0.75 / math.sqrt(width)
    weight = 64.0 * width / math.sqrt(rows * seq_count)
    around, reverse, swap = ring_routes(seq_count)
    hops = seq_count // CORES - 2
    share = rows // pair_count
    pieces = list(pack_share(student, teacher, pair_index, share, split(share, CHAINS)))
    own_half, s_scale = normalize_own(after(student, *pieces), teacher)

    def add(batch, total, **options):
        return add_relation(own_half, batch, [] if total is None else [total], margin, weight, **options)

    def move(x, route, *wait_for):
        return lax.ppermute(after(x, *wait_for), "seq", route)

    batch = pieces + [move(x, swap) for x in pieces]
    totals = []
    held = list(pieces)
    doubled = pair_count == 2
    for event in range(CHAINS * hops):
        k = event % CHAINS
        held[k] = move(held[k], around, *(totals[-1 - LAG :][:1] if len(totals) > LAG else []))
        if event >= FIRST:
            totals.append(add(batch, totals[-1] if totals else None))
            batch = []
        slag = SLAG
        batch += [held[k], move(held[k], swap, *totals[len(totals) - 1 - slag :][:1] if len(totals) > slag else [])]
    if not doubled:
        nearest = [move(x, reverse) for x in pieces]
        batch += nearest + [move(x, swap) for x in nearest]
    own = add(batch, totals[-1], project=(student, s_scale), dtype=jnp.bfloat16)
    summands, distance = (own,), 1
    while distance < pair_count:
        value = sum(x.astype(jnp.float32) for x in summands).astype(jnp.bfloat16)
        route = [(i, i ^ distance) for i in range(pair_count)]
        summands = (value, lax.ppermute(value, "pair", route))
        distance *= 2
    summed = sum(x.astype(jnp.float32) for x in summands)
    if not doubled:
        return s_scale * summed

    nearest, at = [], 0
    for k, n in enumerate(split(rows, PARTS)):
        piece = own_half[:, at : at + n].reshape(2 * n, width)
        nearest.append(move(piece, reverse, own if k else held[0]))
        at += n
    batch = []
    for x in nearest[:-1]:
        batch += [x, move(x, swap, own)]
    total = add(batch, None)
    batch = [nearest[-1], move(nearest[-1], swap)]
    total = add(batch, total, project=(student, s_scale))
    return s_scale * (summed + total)


def solution(mesh):
    placed = (P("seq", None), P("seq", None))
    return jax.shard_map(
        local, mesh=mesh, in_specs=placed, out_specs=P("seq", None), check_vma=False
    )
```

```python
import functools
import math

import jax
import jax.numpy as jnp
from jax import lax
from jax.experimental import pallas as pl
from jax.experimental.pallas import tpu as pltpu
from jax.sharding import PartitionSpec as P

CORES = 2
PARTS = 5
CHAINS = 2
LAG = 2
SLAG = 1
FIRST = 2
BFREE = 1
BLAG = 2
COSTW = 1.0
ROW_TILE = 16
VMEM_LIMIT = 32 * 1024 * 1024
FIRST_VMEM_LIMIT = 58 * 1024 * 1024


def normalized(values):
    width = values.shape[1]
    scale = lax.rsqrt(jnp.sum(values * values, axis=1, keepdims=True) + width * 1e-06)
    return scale, (values * scale).astype(jnp.bfloat16)


def own_kernel(student, teacher, half, scale):
    scale[...], half[0] = normalized(student[...])
    _, half[1] = normalized(teacher[...])


def normalize_own(student, teacher):
    rows, width = student.shape
    block = rows // 4
    by_row = pl.BlockSpec((block, width), lambda i: (i, 0))
    return pl.pallas_call(
        own_kernel,
        grid=(rows // block,),
        in_specs=[by_row, by_row],
        out_specs=[
            pl.BlockSpec((2, block, width), lambda i: (0, i, 0)),
            pl.BlockSpec((block, 1), lambda i: (i, 0)),
        ],
        out_shape=[
            jax.ShapeDtypeStruct((2, rows, width), jnp.bfloat16),
            jax.ShapeDtypeStruct((rows, 1), jnp.float32),
        ],
        compiler_params=pltpu.CompilerParams(vmem_limit_bytes=VMEM_LIMIT),
        cost_estimate=pl.CostEstimate(
            flops=6 * rows * width, bytes_accessed=12 * rows * width, transcendentals=2 * rows
        ),
    )(student, teacher)


def pack_kernel(counts, at, which, student, teacher, *packed):
    for out, count in zip(packed, counts):
        out[:count, :] = normalized(student[at : at + count, :])[1]
        out[count:, :] = normalized(teacher[at : at + count, :])[1]
        at += count


def pack_share(student, teacher, pair_index, share, counts, at=0):
    width = student.shape[1]
    mine = pl.BlockSpec((share, width), lambda i, which: (which[0], 0))
    return pl.pallas_call(
        functools.partial(pack_kernel, counts, at),
        grid_spec=pltpu.PrefetchScalarGridSpec(
            num_scalar_prefetch=1,
            grid=(1,),
            in_specs=[mine, mine],
            out_specs=[pl.BlockSpec((2 * n, width), lambda i, which: (0, 0)) for n in counts],
        ),
        out_shape=[jax.ShapeDtypeStruct((2 * n, width), jnp.bfloat16) for n in counts],
        compiler_params=pltpu.CompilerParams(vmem_limit_bytes=FIRST_VMEM_LIMIT),
        cost_estimate=pl.CostEstimate(
            flops=6 * share * width, bytes_accessed=12 * share * width, transcendentals=2 * share
        ),
    )(jnp.reshape(pair_index, (1,)).astype(jnp.int32), student, teacher)


def relation_kernel(margin, weight, counts, terms, project, halves, *refs):
    refs = list(refs)
    rows = refs.pop(0)
    partners = [refs.pop(0) for _ in counts]
    added = [refs.pop(0) for _ in range(terms)]
    student, scale = (refs.pop(0), refs.pop(0)) if project else (None, None)
    summands = [refs.pop(0) for _ in range(halves)]
    out, all_s, all_t = refs

    @pl.when(pl.program_id(0) == 0)
    def _():
        at = 0
        for partner, count in zip(partners, counts):
            all_s[at : at + count, :] = partner[:count, :]
            all_t[at : at + count, :] = partner[count:, :]
            at += count

    contract = (((1,), (1,)), ((), ()))
    s_rel = lax.dot_general(rows[0], all_s[...], contract, preferred_element_type=jnp.float32)
    t_rel = lax.dot_general(rows[1], all_t[...], contract, preferred_element_type=jnp.float32)
    delta = s_rel - t_rel
    shrink = jnp.maximum(delta - margin, 0.0) + jnp.minimum(delta + margin, 0.0)
    relation = (weight * shrink).astype(jnp.bfloat16)
    grad = jnp.dot(relation, all_s[...], preferred_element_type=jnp.float32)
    for term in added:
        grad = grad + term[...].astype(jnp.float32)
    if project:
        unit = student[...] * scale[...]
        grad = grad - unit * jnp.sum(unit * grad, axis=1, keepdims=True)
    if summands:
        others = [x[...].astype(jnp.float32) for x in summands]
        grad = scale[...] * (sum(others[1:], others[0]) + grad)
    out[...] = grad.astype(out.dtype)


def add_relation(half, partners, terms, margin, weight, project=None, summands=(), dtype=jnp.float32):
    _, rows, width = half.shape
    block = rows // 2
    counts = tuple(x.shape[0] // 2 for x in partners)
    tokens = sum(counts)
    by_row = pl.BlockSpec((block, width), lambda i: (i, 0))
    operands = [half] + list(partners) + list(terms)
    specs = [pl.BlockSpec((2, block, width), lambda i: (0, i, 0))]
    specs += [pl.BlockSpec(x.shape, lambda i: (0, 0), pipeline_mode=pl.Buffered(1)) for x in partners]
    specs += [by_row] * len(terms)
    aliases = {1 + len(partners): 0} if terms and dtype == terms[0].dtype else {}
    if project is not None:
        operands += list(project)
        specs += [by_row, pl.BlockSpec((block, 1), lambda i: (i, 0))]
    operands += list(summands)
    specs += [by_row] * len(summands)
    return pl.pallas_call(
        functools.partial(
            relation_kernel, margin, weight, counts, len(terms), project is not None, len(summands)
        ),
        grid=(rows // block,),
        in_specs=specs,
        out_specs=by_row,
        out_shape=jax.ShapeDtypeStruct((rows, width), dtype),
        scratch_shapes=[pltpu.VMEM((tokens, width), jnp.bfloat16)] * 2,
        input_output_aliases=aliases,
        compiler_params=pltpu.CompilerParams(vmem_limit_bytes=VMEM_LIMIT),
        cost_estimate=pl.CostEstimate(
            flops=6 * rows * tokens * width,
            bytes_accessed=(12 * rows + 4 * tokens) * width,
            transcendentals=0,
        ),
    )(*operands)


def ring_routes(count):
    chips = count // CORES
    order = list(range(0, chips, 2)) + list(range(1, chips, 2))[::-1]
    around = []
    for place, chip in enumerate(order):
        following = order[(place + 1) % chips]
        around.append((chip * CORES, following * CORES))
        around.append((following * CORES + 1, chip * CORES + 1))
    return around, [(to, of) for of, to in around], [(i, i ^ 1) for i in range(count)]


def split(tokens, parts):
    tiles = tokens // ROW_TILE
    return [ROW_TILE * (tiles // parts + (k < tiles % parts)) for k in range(parts)]


def after(x, *values):
    return lax.optimization_barrier((x, *values))[0] if values else x


def local(student, teacher):
    rows, width = student.shape
    seq_count = lax.axis_size("seq")
    pair_count = lax.axis_size("pair")
    pair_index = lax.axis_index("pair")
    margin = 0.75 / math.sqrt(width)
    weight = 64.0 * width / math.sqrt(rows * seq_count)
    around, reverse, swap = ring_routes(seq_count)
    hops = seq_count // CORES - 2
    share = rows // pair_count
    counts = split(share, CHAINS)
    pieces, at = [], 0
    for n in counts:
        pieces += pack_share(student, teacher, pair_index, share, [n], at)
        at += n
    own_half, s_scale = normalize_own(after(student, *pieces), teacher)

    def add(batch, total, **options):
        return add_relation(own_half, batch, [] if total is None else [total], margin, weight, **options)

    def move(x, route, *wait_for):
        return lax.ppermute(after(x, *wait_for), "seq", route)

    batch = pieces + [move(x, swap) for x in pieces]
    totals = []
    held = list(pieces)
    doubled = pair_count == 2
    for event in range(CHAINS * hops):
        k = event % CHAINS
        held[k] = move(held[k], around, *(totals[-1 - LAG :][:1] if len(totals) > LAG else []))
        if event >= FIRST:
            totals.append(add(batch, totals[-1] if totals else None))
            batch = []
        slag = SLAG
        batch += [held[k], move(held[k], swap, *totals[len(totals) - 1 - slag :][:1] if len(totals) > slag else [])]
    if not doubled:
        nearest = [move(x, reverse) for x in pieces]
        batch += nearest + [move(x, swap) for x in nearest]
    own = add(batch, totals[-1], project=(student, s_scale), dtype=jnp.bfloat16)
    summands, distance = (own,), 1
    while distance < pair_count:
        value = sum(x.astype(jnp.float32) for x in summands).astype(jnp.bfloat16)
        route = [(i, i ^ distance) for i in range(pair_count)]
        summands = (value, lax.ppermute(value, "pair", route))
        distance *= 2
    summed = sum(x.astype(jnp.float32) for x in summands)
    if not doubled:
        return s_scale * summed

    sums, at = [], 0
    for k, n in enumerate(split(rows, PARTS)):
        piece = own_half[:, at : at + n].reshape(2 * n, width)
        at += n
        last = k == PARTS - 1
        x = move(piece, reverse, *([own] if k >= BFREE else [held[k % CHAINS]]))
        ready = sums[len(sums) - 1 - BLAG :][:1] if len(sums) > BLAG else [own]
        batch = [x, move(x, swap, *ready)]
        sums.append(add(batch, sums[-1] if sums else None, project=(student, s_scale) if last else None))
    return s_scale * (summed + sums[-1])


def solution(mesh):
    placed = (P("seq", None), P("seq", None))
    return jax.shard_map(
        local, mesh=mesh, in_specs=placed, out_specs=P("seq", None), check_vma=False
    )
```

```python
import functools
import math

import jax
import jax.numpy as jnp
from jax import lax
from jax.experimental import pallas as pl
from jax.experimental.pallas import tpu as pltpu
from jax.sharding import PartitionSpec as P

CORES = 2
PARTS = 5
CHAINS = 2
LAG = 2
SLAG = 1
FIRST = 2
BFREE = 1
BLAG = 2
COSTW = 1.0
ROW_TILE = 16
VMEM_LIMIT = 14 * 1024 * 1024
FIRST_VMEM_LIMIT = 58 * 1024 * 1024


def normalized(values):
    width = values.shape[1]
    scale = lax.rsqrt(jnp.sum(values * values, axis=1, keepdims=True) + width * 1e-06)
    return scale, (values * scale).astype(jnp.bfloat16)


def own_kernel(student, teacher, half, scale):
    scale[...], half[0] = normalized(student[...])
    _, half[1] = normalized(teacher[...])


def normalize_own(student, teacher):
    rows, width = student.shape
    block = rows // 4
    by_row = pl.BlockSpec((block, width), lambda i: (i, 0))
    return pl.pallas_call(
        own_kernel,
        grid=(rows // block,),
        in_specs=[by_row, by_row],
        out_specs=[
            pl.BlockSpec((2, block, width), lambda i: (0, i, 0)),
            pl.BlockSpec((block, 1), lambda i: (i, 0)),
        ],
        out_shape=[
            jax.ShapeDtypeStruct((2, rows, width), jnp.bfloat16),
            jax.ShapeDtypeStruct((rows, 1), jnp.float32),
        ],
        compiler_params=pltpu.CompilerParams(vmem_limit_bytes=VMEM_LIMIT),
        cost_estimate=pl.CostEstimate(
            flops=6 * rows * width, bytes_accessed=12 * rows * width, transcendentals=2 * rows
        ),
    )(student, teacher)


def pack_kernel(counts, at, which, student, teacher, *packed):
    for out, count in zip(packed, counts):
        out[:count, :] = normalized(student[at : at + count, :])[1]
        out[count:, :] = normalized(teacher[at : at + count, :])[1]
        at += count


def pack_share(student, teacher, pair_index, share, counts, at=0):
    width = student.shape[1]
    mine = pl.BlockSpec((share, width), lambda i, which: (which[0], 0))
    return pl.pallas_call(
        functools.partial(pack_kernel, counts, at),
        grid_spec=pltpu.PrefetchScalarGridSpec(
            num_scalar_prefetch=1,
            grid=(1,),
            in_specs=[mine, mine],
            out_specs=[pl.BlockSpec((2 * n, width), lambda i, which: (0, 0)) for n in counts],
        ),
        out_shape=[jax.ShapeDtypeStruct((2 * n, width), jnp.bfloat16) for n in counts],
        compiler_params=pltpu.CompilerParams(vmem_limit_bytes=FIRST_VMEM_LIMIT),
        cost_estimate=pl.CostEstimate(
            flops=6 * share * width, bytes_accessed=12 * share * width, transcendentals=2 * share
        ),
    )(jnp.reshape(pair_index, (1,)).astype(jnp.int32), student, teacher)


def relation_kernel(margin, weight, counts, terms, project, halves, *refs):
    refs = list(refs)
    rows = refs.pop(0)
    partners = [refs.pop(0) for _ in counts]
    added = [refs.pop(0) for _ in range(terms)]
    student, scale = (refs.pop(0), refs.pop(0)) if project else (None, None)
    summands = [refs.pop(0) for _ in range(halves)]
    out, all_s, all_t = refs

    @pl.when(pl.program_id(0) == 0)
    def _():
        at = 0
        for partner, count in zip(partners, counts):
            all_s[at : at + count, :] = partner[:count, :]
            all_t[at : at + count, :] = partner[count:, :]
            at += count

    contract = (((1,), (1,)), ((), ()))
    s_rel = lax.dot_general(rows[0], all_s[...], contract, preferred_element_type=jnp.float32)
    t_rel = lax.dot_general(rows[1], all_t[...], contract, preferred_element_type=jnp.float32)
    delta = s_rel - t_rel
    shrink = jnp.maximum(delta - margin, 0.0) + jnp.minimum(delta + margin, 0.0)
    relation = (weight * shrink).astype(jnp.bfloat16)
    grad = jnp.dot(relation, all_s[...], preferred_element_type=jnp.float32)
    for term in added:
        grad = grad + term[...].astype(jnp.float32)
    if project:
        unit = student[...] * scale[...]
        grad = grad - unit * jnp.sum(unit * grad, axis=1, keepdims=True)
    if summands:
        others = [x[...].astype(jnp.float32) for x in summands]
        grad = scale[...] * (sum(others[1:], others[0]) + grad)
    out[...] = grad.astype(out.dtype)


def add_relation(half, partners, terms, margin, weight, project=None, summands=(), dtype=jnp.float32):
    _, rows, width = half.shape
    block = rows // 2
    counts = tuple(x.shape[0] // 2 for x in partners)
    tokens = sum(counts)
    by_row = pl.BlockSpec((block, width), lambda i: (i, 0))
    operands = [half] + list(partners) + list(terms)
    specs = [pl.BlockSpec((2, block, width), lambda i: (0, i, 0))]
    specs += [pl.BlockSpec(x.shape, lambda i: (0, 0), pipeline_mode=pl.Buffered(1)) for x in partners]
    specs += [by_row] * len(terms)
    aliases = {1 + len(partners): 0} if terms and dtype == terms[0].dtype else {}
    if project is not None:
        operands += list(project)
        specs += [by_row, pl.BlockSpec((block, 1), lambda i: (i, 0))]
    operands += list(summands)
    specs += [by_row] * len(summands)
    return pl.pallas_call(
        functools.partial(
            relation_kernel, margin, weight, counts, len(terms), project is not None, len(summands)
        ),
        grid=(rows // block,),
        in_specs=specs,
        out_specs=by_row,
        out_shape=jax.ShapeDtypeStruct((rows, width), dtype),
        scratch_shapes=[pltpu.VMEM((tokens, width), jnp.bfloat16)] * 2,
        input_output_aliases=aliases,
        compiler_params=pltpu.CompilerParams(vmem_limit_bytes=VMEM_LIMIT),
        cost_estimate=pl.CostEstimate(
            flops=6 * rows * tokens * width,
            bytes_accessed=(12 * rows + 4 * tokens) * width,
            transcendentals=0,
        ),
    )(*operands)


def ring_routes(count):
    chips = count // CORES
    order = list(range(0, chips, 2)) + list(range(1, chips, 2))[::-1]
    around = []
    for place, chip in enumerate(order):
        following = order[(place + 1) % chips]
        around.append((chip * CORES, following * CORES))
        around.append((following * CORES + 1, chip * CORES + 1))
    return around, [(to, of) for of, to in around], [(i, i ^ 1) for i in range(count)]


def split(tokens, parts):
    tiles = tokens // ROW_TILE
    return [ROW_TILE * (tiles // parts + (k < tiles % parts)) for k in range(parts)]


def after(x, *values):
    return lax.optimization_barrier((x, *values))[0] if values else x


def local(student, teacher):
    rows, width = student.shape
    seq_count = lax.axis_size("seq")
    pair_count = lax.axis_size("pair")
    pair_index = lax.axis_index("pair")
    margin = 0.75 / math.sqrt(width)
    weight = 64.0 * width / math.sqrt(rows * seq_count)
    around, reverse, swap = ring_routes(seq_count)
    hops = seq_count // CORES - 2
    share = rows // pair_count
    counts = split(share, CHAINS)
    pieces, at = [], 0
    for n in counts:
        pieces += pack_share(student, teacher, pair_index, share, [n], at)
        at += n
    own_half, s_scale = normalize_own(after(student, *pieces), teacher)

    def add(batch, total, **options):
        return add_relation(own_half, batch, [] if total is None else [total], margin, weight, **options)

    def move(x, route, *wait_for):
        return lax.ppermute(after(x, *wait_for), "seq", route)

    batch = pieces + [move(x, swap) for x in pieces]
    totals = []
    held = list(pieces)
    doubled = pair_count == 2
    for event in range(CHAINS * hops):
        k = event % CHAINS
        held[k] = move(held[k], around, *(totals[-1 - LAG :][:1] if len(totals) > LAG else []))
        if event >= FIRST:
            totals.append(add(batch, totals[-1] if totals else None))
            batch = []
        slag = SLAG
        batch += [held[k], move(held[k], swap, *totals[len(totals) - 1 - slag :][:1] if len(totals) > slag else [])]
    if not doubled:
        nearest = [move(x, reverse) for x in pieces]
        batch += nearest + [move(x, swap) for x in nearest]
    own = add(batch, totals[-1], project=(student, s_scale), dtype=jnp.bfloat16)
    summands, distance = (own,), 1
    while distance < pair_count:
        value = sum(x.astype(jnp.float32) for x in summands).astype(jnp.bfloat16)
        route = [(i, i ^ distance) for i in range(pair_count)]
        summands = (value, lax.ppermute(value, "pair", route))
        distance *= 2
    summed = sum(x.astype(jnp.float32) for x in summands)
    if not doubled:
        return s_scale * summed

    sums, at = [], 0
    for k, n in enumerate(split(rows, PARTS)):
        piece = own_half[:, at : at + n].reshape(2 * n, width)
        at += n
        last = k == PARTS - 1
        x = move(piece, reverse, *([own] if k >= BFREE else [held[k % CHAINS]]))
        ready = sums[len(sums) - 1 - BLAG :][:1] if len(sums) > BLAG else [own]
        batch = [x, move(x, swap, *ready)]
        sums.append(add(batch, sums[-1] if sums else None, project=(student, s_scale) if last else None))
    return s_scale * (summed + sums[-1])


def solution(mesh):
    placed = (P("seq", None), P("seq", None))
    return jax.shard_map(
        local, mesh=mesh, in_specs=placed, out_specs=P("seq", None), check_vma=False
    )
```

```python
import functools
import math

import jax
import jax.numpy as jnp
from jax import lax
from jax.experimental import pallas as pl
from jax.experimental.pallas import tpu as pltpu
from jax.sharding import PartitionSpec as P

CORES = 2
PARTS = 4
CHAINS = 2
LAG = 2
SLAG = 1
FIRST = 2
COSTW = 1.0
ROW_TILE = 16
VMEM_LIMIT = 32 * 1024 * 1024
FIRST_VMEM_LIMIT = 58 * 1024 * 1024


def normalized(values):
    width = values.shape[1]
    scale = lax.rsqrt(jnp.sum(values * values, axis=1, keepdims=True) + width * 1e-06)
    return scale, (values * scale).astype(jnp.bfloat16)


def own_kernel(student, teacher, half, scale):
    scale[...], half[0] = normalized(student[...])
    _, half[1] = normalized(teacher[...])


def normalize_own(student, teacher):
    rows, width = student.shape
    block = rows // 4
    by_row = pl.BlockSpec((block, width), lambda i: (i, 0))
    return pl.pallas_call(
        own_kernel,
        grid=(rows // block,),
        in_specs=[by_row, by_row],
        out_specs=[
            pl.BlockSpec((2, block, width), lambda i: (0, i, 0)),
            pl.BlockSpec((block, 1), lambda i: (i, 0)),
        ],
        out_shape=[
            jax.ShapeDtypeStruct((2, rows, width), jnp.bfloat16),
            jax.ShapeDtypeStruct((rows, 1), jnp.float32),
        ],
        compiler_params=pltpu.CompilerParams(vmem_limit_bytes=VMEM_LIMIT),
        cost_estimate=pl.CostEstimate(
            flops=6 * rows * width, bytes_accessed=12 * rows * width, transcendentals=2 * rows
        ),
    )(student, teacher)


def pack_kernel(counts, which, student, teacher, *packed):
    at = 0
    for out, count in zip(packed, counts):
        out[:count, :] = normalized(student[at : at + count, :])[1]
        out[count:, :] = normalized(teacher[at : at + count, :])[1]
        at += count


def pack_share(student, teacher, pair_index, share, counts):
    width = student.shape[1]
    mine = pl.BlockSpec((share, width), lambda i, which: (which[0], 0))
    return pl.pallas_call(
        functools.partial(pack_kernel, counts),
        grid_spec=pltpu.PrefetchScalarGridSpec(
            num_scalar_prefetch=1,
            grid=(1,),
            in_specs=[mine, mine],
            out_specs=[pl.BlockSpec((2 * n, width), lambda i, which: (0, 0)) for n in counts],
        ),
        out_shape=[jax.ShapeDtypeStruct((2 * n, width), jnp.bfloat16) for n in counts],
        compiler_params=pltpu.CompilerParams(vmem_limit_bytes=FIRST_VMEM_LIMIT),
        cost_estimate=pl.CostEstimate(
            flops=6 * share * width, bytes_accessed=12 * share * width, transcendentals=2 * share
        ),
    )(jnp.reshape(pair_index, (1,)).astype(jnp.int32), student, teacher)


def relation_kernel(margin, weight, counts, terms, project, halves, *refs):
    refs = list(refs)
    rows = refs.pop(0)
    partners = [refs.pop(0) for _ in counts]
    added = [refs.pop(0) for _ in range(terms)]
    student, scale = (refs.pop(0), refs.pop(0)) if project else (None, None)
    summands = [refs.pop(0) for _ in range(halves)]
    out, all_s, all_t = refs

    @pl.when(pl.program_id(0) == 0)
    def _():
        at = 0
        for partner, count in zip(partners, counts):
            all_s[at : at + count, :] = partner[:count, :]
            all_t[at : at + count, :] = partner[count:, :]
            at += count

    contract = (((1,), (1,)), ((), ()))
    s_rel = lax.dot_general(rows[0], all_s[...], contract, preferred_element_type=jnp.float32)
    t_rel = lax.dot_general(rows[1], all_t[...], contract, preferred_element_type=jnp.float32)
    delta = s_rel - t_rel
    shrink = jnp.maximum(delta - margin, 0.0) + jnp.minimum(delta + margin, 0.0)
    relation = (weight * shrink).astype(jnp.bfloat16)
    grad = jnp.dot(relation, all_s[...], preferred_element_type=jnp.float32)
    for term in added:
        grad = grad + term[...].astype(jnp.float32)
    if project:
        unit = student[...] * scale[...]
        grad = grad - unit * jnp.sum(unit * grad, axis=1, keepdims=True)
    if summands:
        others = [x[...].astype(jnp.float32) for x in summands]
        grad = scale[...] * (sum(others[1:], others[0]) + grad)
    out[...] = grad.astype(out.dtype)


def add_relation(half, partners, terms, margin, weight, project=None, summands=(), dtype=jnp.float32):
    _, rows, width = half.shape
    block = rows // 2
    counts = tuple(x.shape[0] // 2 for x in partners)
    tokens = sum(counts)
    by_row = pl.BlockSpec((block, width), lambda i: (i, 0))
    operands = [half] + list(partners) + list(terms)
    specs = [pl.BlockSpec((2, block, width), lambda i: (0, i, 0))]
    specs += [pl.BlockSpec(x.shape, lambda i: (0, 0), pipeline_mode=pl.Buffered(1)) for x in partners]
    specs += [by_row] * len(terms)
    aliases = {1 + len(partners): 0} if terms and dtype == terms[0].dtype else {}
    if project is not None:
        operands += list(project)
        specs += [by_row, pl.BlockSpec((block, 1), lambda i: (i, 0))]
    operands += list(summands)
    specs += [by_row] * len(summands)
    return pl.pallas_call(
        functools.partial(
            relation_kernel, margin, weight, counts, len(terms), project is not None, len(summands)
        ),
        grid=(rows // block,),
        in_specs=specs,
        out_specs=by_row,
        out_shape=jax.ShapeDtypeStruct((rows, width), dtype),
        scratch_shapes=[pltpu.VMEM((tokens, width), jnp.bfloat16)] * 2,
        input_output_aliases=aliases,
        compiler_params=pltpu.CompilerParams(vmem_limit_bytes=VMEM_LIMIT),
        cost_estimate=pl.CostEstimate(
            flops=6 * rows * tokens * width,
            bytes_accessed=(12 * rows + 4 * tokens) * width,
            transcendentals=0,
        ),
    )(*operands)


def ring_routes(count):
    chips = count // CORES
    order = list(range(0, chips, 2)) + list(range(1, chips, 2))[::-1]
    around = []
    for place, chip in enumerate(order):
        following = order[(place + 1) % chips]
        around.append((chip * CORES, following * CORES))
        around.append((following * CORES + 1, chip * CORES + 1))
    return around, [(to, of) for of, to in around], [(i, i ^ 1) for i in range(count)]


def split(tokens, parts):
    tiles = tokens // ROW_TILE
    return [ROW_TILE * (tiles // parts + (k < tiles % parts)) for k in range(parts)]


def after(x, *values):
    return lax.optimization_barrier((x, *values))[0] if values else x


def local(student, teacher):
    rows, width = student.shape
    seq_count = lax.axis_size("seq")
    pair_count = lax.axis_size("pair")
    pair_index = lax.axis_index("pair")
    margin = 0.75 / math.sqrt(width)
    weight = 64.0 * width / math.sqrt(rows * seq_count)
    around, reverse, swap = ring_routes(seq_count)
    hops = seq_count // CORES - 2
    share = rows // pair_count
    pieces = list(pack_share(student, teacher, pair_index, share, split(share, CHAINS)))
    own_half, s_scale = normalize_own(after(student, *pieces), teacher)

    def add(batch, total, **options):
        return add_relation(own_half, batch, [] if total is None else [total], margin, weight, **options)

    def move(x, route, *wait_for):
        return lax.ppermute(after(x, *wait_for), "seq", route)

    batch = pieces + [move(x, swap) for x in pieces]
    totals = []
    held = list(pieces)
    doubled = pair_count == 2
    for event in range(CHAINS * hops):
        k = event % CHAINS
        held[k] = move(held[k], around, *(totals[-1 - LAG :][:1] if len(totals) > LAG else []))
        if event >= FIRST:
            totals.append(add(batch, totals[-1] if totals else None))
            batch = []
        slag = SLAG
        batch += [held[k], move(held[k], swap, *totals[len(totals) - 1 - slag :][:1] if len(totals) > slag else [])]
    if not doubled:
        nearest = [move(x, reverse) for x in pieces]
        batch += nearest + [move(x, swap) for x in nearest]
    own = add(batch, totals[-1], project=(student, s_scale), dtype=jnp.bfloat16)
    summands, distance = (own,), 1
    while distance < pair_count:
        value = sum(x.astype(jnp.float32) for x in summands).astype(jnp.bfloat16)
        route = [(i, i ^ distance) for i in range(pair_count)]
        summands = (value, lax.ppermute(value, "pair", route))
        distance *= 2
    if not doubled:
        return s_scale * sum(x.astype(jnp.float32) for x in summands)

    nearest, at = [], 0
    for k, n in enumerate(split(rows, PARTS)):
        piece = own_half[:, at : at + n].reshape(2 * n, width)
        nearest.append(move(piece, reverse, own if k else held[0]))
        at += n
    batch = []
    for x in nearest[:-1]:
        batch += [x, move(x, swap, own)]
    total = add(batch, None)
    batch = [nearest[-1], move(nearest[-1], swap)]
    return add(batch, total, project=(student, s_scale), summands=summands)


def solution(mesh):
    placed = (P("seq", None), P("seq", None))
    return jax.shard_map(
        local, mesh=mesh, in_specs=placed, out_specs=P("seq", None), check_vma=False
    )
```

```python
import functools
import math

import jax
import jax.numpy as jnp
from jax import lax
from jax.experimental import pallas as pl
from jax.experimental.pallas import tpu as pltpu
from jax.sharding import PartitionSpec as P

CORES = 2
PARTS = 4
CHAINS = 2
LAG = 2
SLAG = 1
FIRST = 2
COSTW = 1.0
ROW_TILE = 16
VMEM_LIMIT = 32 * 1024 * 1024
FIRST_VMEM_LIMIT = 58 * 1024 * 1024


def normalized(values):
    width = values.shape[1]
    scale = lax.rsqrt(jnp.sum(values * values, axis=1, keepdims=True) + width * 1e-06)
    return scale, (values * scale).astype(jnp.bfloat16)


def own_kernel(student, teacher, half, scale):
    scale[...], half[0] = normalized(student[...])
    _, half[1] = normalized(teacher[...])


def normalize_own(student, teacher):
    rows, width = student.shape
    block = rows // 4
    by_row = pl.BlockSpec((block, width), lambda i: (i, 0))
    return pl.pallas_call(
        own_kernel,
        grid=(rows // block,),
        in_specs=[by_row, by_row],
        out_specs=[
            pl.BlockSpec((2, block, width), lambda i: (0, i, 0)),
            pl.BlockSpec((block, 1), lambda i: (i, 0)),
        ],
        out_shape=[
            jax.ShapeDtypeStruct((2, rows, width), jnp.bfloat16),
            jax.ShapeDtypeStruct((rows, 1), jnp.float32),
        ],
        compiler_params=pltpu.CompilerParams(vmem_limit_bytes=VMEM_LIMIT),
        cost_estimate=pl.CostEstimate(
            flops=6 * rows * width, bytes_accessed=12 * rows * width, transcendentals=2 * rows
        ),
    )(student, teacher)


def pack_kernel(counts, which, student, teacher, *packed):
    at = 0
    for out, count in zip(packed, counts):
        out[:count, :] = normalized(student[at : at + count, :])[1]
        out[count:, :] = normalized(teacher[at : at + count, :])[1]
        at += count


def pack_share(student, teacher, pair_index, share, counts):
    width = student.shape[1]
    mine = pl.BlockSpec((share, width), lambda i, which: (which[0], 0))
    return pl.pallas_call(
        functools.partial(pack_kernel, counts),
        grid_spec=pltpu.PrefetchScalarGridSpec(
            num_scalar_prefetch=1,
            grid=(1,),
            in_specs=[mine, mine],
            out_specs=[pl.BlockSpec((2 * n, width), lambda i, which: (0, 0)) for n in counts],
        ),
        out_shape=[jax.ShapeDtypeStruct((2 * n, width), jnp.bfloat16) for n in counts],
        compiler_params=pltpu.CompilerParams(vmem_limit_bytes=FIRST_VMEM_LIMIT),
        cost_estimate=pl.CostEstimate(
            flops=6 * share * width, bytes_accessed=12 * share * width, transcendentals=2 * share
        ),
    )(jnp.reshape(pair_index, (1,)).astype(jnp.int32), student, teacher)


def relation_kernel(margin, weight, counts, terms, project, halves, *refs):
    refs = list(refs)
    rows = refs.pop(0)
    partners = [refs.pop(0) for _ in counts]
    added = [refs.pop(0) for _ in range(terms)]
    student, scale = (refs.pop(0), refs.pop(0)) if project else (None, None)
    summands = [refs.pop(0) for _ in range(halves)]
    out, all_s, all_t = refs

    @pl.when(pl.program_id(0) == 0)
    def _():
        at = 0
        for partner, count in zip(partners, counts):
            all_s[at : at + count, :] = partner[:count, :]
            all_t[at : at + count, :] = partner[count:, :]
            at += count

    contract = (((1,), (1,)), ((), ()))
    s_rel = lax.dot_general(rows[0], all_s[...], contract, preferred_element_type=jnp.float32)
    t_rel = lax.dot_general(rows[1], all_t[...], contract, preferred_element_type=jnp.float32)
    delta = s_rel - t_rel
    shrink = jnp.maximum(delta - margin, 0.0) + jnp.minimum(delta + margin, 0.0)
    relation = (weight * shrink).astype(jnp.bfloat16)
    grad = jnp.dot(relation, all_s[...], preferred_element_type=jnp.float32)
    for term in added:
        grad = grad + term[...].astype(jnp.float32)
    if project:
        unit = student[...] * scale[...]
        grad = grad - unit * jnp.sum(unit * grad, axis=1, keepdims=True)
    if summands:
        others = [x[...].astype(jnp.float32) for x in summands]
        grad = scale[...] * (sum(others[1:], others[0]) + grad)
    out[...] = grad.astype(out.dtype)


def add_relation(half, partners, terms, margin, weight, project=None, summands=(), dtype=jnp.float32):
    _, rows, width = half.shape
    block = rows // 2
    counts = tuple(x.shape[0] // 2 for x in partners)
    tokens = sum(counts)
    by_row = pl.BlockSpec((block, width), lambda i: (i, 0))
    operands = [half] + list(partners) + list(terms)
    specs = [pl.BlockSpec((2, block, width), lambda i: (0, i, 0))]
    specs += [pl.BlockSpec(x.shape, lambda i: (0, 0), pipeline_mode=pl.Buffered(1)) for x in partners]
    specs += [by_row] * len(terms)
    aliases = {1 + len(partners): 0} if terms and dtype == terms[0].dtype else {}
    if project is not None:
        operands += list(project)
        specs += [by_row, pl.BlockSpec((block, 1), lambda i: (i, 0))]
    operands += list(summands)
    specs += [by_row] * len(summands)
    return pl.pallas_call(
        functools.partial(
            relation_kernel, margin, weight, counts, len(terms), project is not None, len(summands)
        ),
        grid=(rows // block,),
        in_specs=specs,
        out_specs=by_row,
        out_shape=jax.ShapeDtypeStruct((rows, width), dtype),
        scratch_shapes=[pltpu.VMEM((tokens, width), jnp.bfloat16)] * 2,
        input_output_aliases=aliases,
        compiler_params=pltpu.CompilerParams(vmem_limit_bytes=VMEM_LIMIT),
        cost_estimate=pl.CostEstimate(
            flops=6 * rows * tokens * width,
            bytes_accessed=(12 * rows + 4 * tokens) * width,
            transcendentals=0,
        ),
    )(*operands)


def ring_routes(count):
    chips = count // CORES
    order = list(range(0, chips, 2)) + list(range(1, chips, 2))[::-1]
    around = []
    for place, chip in enumerate(order):
        following = order[(place + 1) % chips]
        around.append((chip * CORES, following * CORES))
        around.append((following * CORES + 1, chip * CORES + 1))
    return around, [(to, of) for of, to in around], [(i, i ^ 1) for i in range(count)]


def split(tokens, parts):
    tiles = tokens // ROW_TILE
    return [ROW_TILE * (tiles // parts + (k < tiles % parts)) for k in range(parts)]


def after(x, *values):
    return lax.optimization_barrier((x, *values))[0] if values else x


def local(student, teacher):
    rows, width = student.shape
    seq_count = lax.axis_size("seq")
    pair_count = lax.axis_size("pair")
    pair_index = lax.axis_index("pair")
    margin = 0.75 / math.sqrt(width)
    weight = 64.0 * width / math.sqrt(rows * seq_count)
    around, reverse, swap = ring_routes(seq_count)
    hops = seq_count // CORES - 2
    share = rows // pair_count
    pieces = list(pack_share(student, teacher, pair_index, share, split(share, CHAINS)))
    own_half, s_scale = normalize_own(after(student, *pieces), teacher)

    def add(batch, total, **options):
        return add_relation(own_half, batch, [] if total is None else [total], margin, weight, **options)

    def move(x, route, *wait_for):
        return lax.ppermute(after(x, *wait_for), "seq", route)

    batch = pieces + [move(x, swap) for x in pieces]
    totals = []
    held = list(pieces)
    doubled = pair_count == 2
    for event in range(CHAINS * hops):
        k = event % CHAINS
        held[k] = move(held[k], around, *(totals[-1 - LAG :][:1] if len(totals) > LAG else []))
        if event >= FIRST:
            totals.append(add(batch, totals[-1] if totals else None))
            batch = []
        slag = SLAG
        batch += [held[k], move(held[k], swap, *totals[len(totals) - 1 - slag :][:1] if len(totals) > slag else [])]
    if not doubled:
        nearest = [move(x, reverse) for x in pieces]
        batch += nearest + [move(x, swap) for x in nearest]
    own = add(batch, totals[-1], project=(student, s_scale), dtype=jnp.bfloat16)
    summands, distance = (own,), 1
    while distance < pair_count:
        value = sum(x.astype(jnp.float32) for x in summands).astype(jnp.bfloat16)
        route = [(i, i ^ distance) for i in range(pair_count)]
        summands = (value, lax.ppermute(value, "pair", route))
        distance *= 2
    if not doubled:
        return s_scale * sum(x.astype(jnp.float32) for x in summands)

    nearest, at = [], 0
    for k, n in enumerate(split(rows, PARTS)):
        piece = own_half[:, at : at + n].reshape(2 * n, width)
        nearest.append(move(piece, reverse, own if k else held[0]))
        at += n
    batch = nearest + [move(x, swap, own) for x in nearest]
    total = add(batch, None, project=(student, s_scale))
    return s_scale * (sum(x.astype(jnp.float32) for x in summands) + total)


def solution(mesh):
    placed = (P("seq", None), P("seq", None))
    return jax.shard_map(
        local, mesh=mesh, in_specs=placed, out_specs=P("seq", None), check_vma=False
    )
```

```python
import functools
import math

import jax
import jax.numpy as jnp
from jax import lax
from jax.experimental import pallas as pl
from jax.experimental.pallas import tpu as pltpu
from jax.sharding import PartitionSpec as P

CORES = 2
PARTS = 4
CHAINS = 2
LAG = 2
SLAG = 1
FIRST = 2
COSTW = 1.0
ROW_TILE = 16
VMEM_LIMIT = 32 * 1024 * 1024
FIRST_VMEM_LIMIT = 58 * 1024 * 1024


def normalized(values):
    width = values.shape[1]
    scale = lax.rsqrt(jnp.sum(values * values, axis=1, keepdims=True) + width * 1e-06)
    return scale, (values * scale).astype(jnp.bfloat16)


def own_kernel(student, teacher, half, scale):
    scale[...], half[0] = normalized(student[...])
    _, half[1] = normalized(teacher[...])


def normalize_own(student, teacher):
    rows, width = student.shape
    block = rows // 4
    by_row = pl.BlockSpec((block, width), lambda i: (i, 0))
    return pl.pallas_call(
        own_kernel,
        grid=(rows // block,),
        in_specs=[by_row, by_row],
        out_specs=[
            pl.BlockSpec((2, block, width), lambda i: (0, i, 0)),
            pl.BlockSpec((block, 1), lambda i: (i, 0)),
        ],
        out_shape=[
            jax.ShapeDtypeStruct((2, rows, width), jnp.bfloat16),
            jax.ShapeDtypeStruct((rows, 1), jnp.float32),
        ],
        compiler_params=pltpu.CompilerParams(vmem_limit_bytes=VMEM_LIMIT),
        cost_estimate=pl.CostEstimate(
            flops=6 * rows * width, bytes_accessed=12 * rows * width, transcendentals=2 * rows
        ),
    )(student, teacher)


def pack_kernel(counts, which, student, teacher, *packed):
    at = 0
    for out, count in zip(packed, counts):
        out[:count, :] = normalized(student[at : at + count, :])[1]
        out[count:, :] = normalized(teacher[at : at + count, :])[1]
        at += count


def pack_share(student, teacher, pair_index, share, counts):
    width = student.shape[1]
    mine = pl.BlockSpec((share, width), lambda i, which: (which[0], 0))
    return pl.pallas_call(
        functools.partial(pack_kernel, counts),
        grid_spec=pltpu.PrefetchScalarGridSpec(
            num_scalar_prefetch=1,
            grid=(1,),
            in_specs=[mine, mine],
            out_specs=[pl.BlockSpec((2 * n, width), lambda i, which: (0, 0)) for n in counts],
        ),
        out_shape=[jax.ShapeDtypeStruct((2 * n, width), jnp.bfloat16) for n in counts],
        compiler_params=pltpu.CompilerParams(vmem_limit_bytes=FIRST_VMEM_LIMIT),
        cost_estimate=pl.CostEstimate(
            flops=6 * share * width, bytes_accessed=12 * share * width, transcendentals=2 * share
        ),
    )(jnp.reshape(pair_index, (1,)).astype(jnp.int32), student, teacher)


def relation_kernel(margin, weight, counts, terms, project, halves, *refs):
    refs = list(refs)
    rows = refs.pop(0)
    partners = [refs.pop(0) for _ in counts]
    added = [refs.pop(0) for _ in range(terms)]
    student, scale = (refs.pop(0), refs.pop(0)) if project else (None, None)
    summands = [refs.pop(0) for _ in range(halves)]
    out, all_s, all_t = refs

    @pl.when(pl.program_id(0) == 0)
    def _():
        at = 0
        for partner, count in zip(partners, counts):
            all_s[at : at + count, :] = partner[:count, :]
            all_t[at : at + count, :] = partner[count:, :]
            at += count

    contract = (((1,), (1,)), ((), ()))
    s_rel = lax.dot_general(rows[0], all_s[...], contract, preferred_element_type=jnp.float32)
    t_rel = lax.dot_general(rows[1], all_t[...], contract, preferred_element_type=jnp.float32)
    delta = s_rel - t_rel
    shrink = jnp.maximum(delta - margin, 0.0) + jnp.minimum(delta + margin, 0.0)
    relation = (weight * shrink).astype(jnp.bfloat16)
    grad = jnp.dot(relation, all_s[...], preferred_element_type=jnp.float32)
    for term in added:
        grad = grad + term[...].astype(jnp.float32)
    if project:
        unit = student[...] * scale[...]
        grad = grad - unit * jnp.sum(unit * grad, axis=1, keepdims=True)
    if summands:
        others = [x[...].astype(jnp.float32) for x in summands]
        grad = scale[...] * (sum(others[1:], others[0]) + grad)
    out[...] = grad.astype(out.dtype)


def add_relation(half, partners, terms, margin, weight, project=None, summands=(), dtype=jnp.float32):
    _, rows, width = half.shape
    block = rows // (2 if project is None else 4)
    counts = tuple(x.shape[0] // 2 for x in partners)
    tokens = sum(counts)
    by_row = pl.BlockSpec((block, width), lambda i: (i, 0))
    operands = [half] + list(partners) + list(terms)
    specs = [pl.BlockSpec((2, block, width), lambda i: (0, i, 0))]
    specs += [pl.BlockSpec(x.shape, lambda i: (0, 0), pipeline_mode=pl.Buffered(1)) for x in partners]
    specs += [by_row] * len(terms)
    aliases = {1 + len(partners): 0} if terms and dtype == terms[0].dtype else {}
    if project is not None:
        operands += list(project)
        specs += [by_row, pl.BlockSpec((block, 1), lambda i: (i, 0))]
    operands += list(summands)
    specs += [by_row] * len(summands)
    return pl.pallas_call(
        functools.partial(
            relation_kernel, margin, weight, counts, len(terms), project is not None, len(summands)
        ),
        grid=(rows // block,),
        in_specs=specs,
        out_specs=by_row,
        out_shape=jax.ShapeDtypeStruct((rows, width), dtype),
        scratch_shapes=[pltpu.VMEM((tokens, width), jnp.bfloat16)] * 2,
        input_output_aliases=aliases,
        compiler_params=pltpu.CompilerParams(vmem_limit_bytes=VMEM_LIMIT),
        cost_estimate=pl.CostEstimate(
            flops=6 * rows * tokens * width,
            bytes_accessed=(12 * rows + 4 * tokens) * width,
            transcendentals=0,
        ),
    )(*operands)


def ring_routes(count):
    chips = count // CORES
    order = list(range(0, chips, 2)) + list(range(1, chips, 2))[::-1]
    around = []
    for place, chip in enumerate(order):
        following = order[(place + 1) % chips]
        around.append((chip * CORES, following * CORES))
        around.append((following * CORES + 1, chip * CORES + 1))
    return around, [(to, of) for of, to in around], [(i, i ^ 1) for i in range(count)]


def split(tokens, parts):
    tiles = tokens // ROW_TILE
    return [ROW_TILE * (tiles // parts + (k < tiles % parts)) for k in range(parts)]


def after(x, *values):
    return lax.optimization_barrier((x, *values))[0] if values else x


def local(student, teacher):
    rows, width = student.shape
    seq_count = lax.axis_size("seq")
    pair_count = lax.axis_size("pair")
    pair_index = lax.axis_index("pair")
    margin = 0.75 / math.sqrt(width)
    weight = 64.0 * width / math.sqrt(rows * seq_count)
    around, reverse, swap = ring_routes(seq_count)
    hops = seq_count // CORES - 2
    share = rows // pair_count
    pieces = list(pack_share(student, teacher, pair_index, share, split(share, CHAINS)))
    own_half, s_scale = normalize_own(after(student, *pieces), teacher)

    def add(batch, total, **options):
        return add_relation(own_half, batch, [] if total is None else [total], margin, weight, **options)

    def move(x, route, *wait_for):
        return lax.ppermute(after(x, *wait_for), "seq", route)

    batch = pieces + [move(x, swap) for x in pieces]
    totals = []
    held = list(pieces)
    doubled = pair_count == 2
    for event in range(CHAINS * hops):
        k = event % CHAINS
        held[k] = move(held[k], around, *(totals[-1 - LAG :][:1] if len(totals) > LAG else []))
        if event >= FIRST:
            totals.append(add(batch, totals[-1] if totals else None))
            batch = []
        slag = SLAG
        batch += [held[k], move(held[k], swap, *totals[len(totals) - 1 - slag :][:1] if len(totals) > slag else [])]
    if not doubled:
        nearest = [move(x, reverse) for x in pieces]
        batch += nearest + [move(x, swap) for x in nearest]
    own = add(batch, totals[-1], project=(student, s_scale), dtype=jnp.bfloat16)
    summands, distance = (own,), 1
    while distance < pair_count:
        value = sum(x.astype(jnp.float32) for x in summands).astype(jnp.bfloat16)
        route = [(i, i ^ distance) for i in range(pair_count)]
        summands = (value, lax.ppermute(value, "pair", route))
        distance *= 2
    if not doubled:
        return s_scale * sum(x.astype(jnp.float32) for x in summands)

    nearest, at = [], 0
    for k, n in enumerate(split(rows, PARTS)):
        piece = own_half[:, at : at + n].reshape(2 * n, width)
        nearest.append(move(piece, reverse, own if k else held[0]))
        at += n
    batch = []
    for x in nearest[:-1]:
        batch += [x, move(x, swap, own)]
    total = add(batch, None)
    batch = [nearest[-1], move(nearest[-1], swap)]
    return add(batch, total, project=(student, s_scale), summands=summands)


def solution(mesh):
    placed = (P("seq", None), P("seq", None))
    return jax.shard_map(
        local, mesh=mesh, in_specs=placed, out_specs=P("seq", None), check_vma=False
    )
```
